32 devices in a mesh: shard: 2 (over y), ctx: 4 (over z), tp: 4 (over x, core).
Axes of the slice: x: 2, y: 2, z: 4, core: 2. Of those that a mesh axis runs over, the one named last changes fastest.
Arguments:
- tokens: bfloat16 [4, 256, 4, 1024], P('shard', None, 'ctx'), may hold values from -6 to 6
- cotangent: bfloat16 [4, 256, 4, 1024], P('shard', None, 'ctx'), may hold values from -6 to 6
- norm_gain: bfloat16 [2, 1024], replicated, may hold values from 0.25 to 1.75
- norm_bias: bfloat16 [2, 1024], replicated, may hold values from -1 to 1
- w_qkv: bfloat16 [1024, 3, 1024], P('shard', None, 'tp'), may hold values from -0.1875 to 0.1875
- qv_bias: bfloat16 [2, 1024], P(None, 'tp'), may hold values from -1 to 1
- w_out: bfloat16 [1024, 1024], P('shard', 'tp'), may hold values from -0.75 to 0.75
- out_bias: bfloat16 [2, 1024], replicated, may hold values from -2.5 to 2.5
- w_up: bfloat16 [1024, 4096], P('shard', 'tp'), may hold values from -0.1875 to 0.1875
- hidden_bias: bfloat16 [4096], P('tp'), may hold values from -1 to 1
- w_down: bfloat16 [1024, 4096], P('shard', 'tp'), may hold values from -0.09375 to 0.09375
Outputs:
- mixed: bfloat16 [4, 256, 4, 1024], P('shard', None, 'ctx')
- input_grad: float32 [4, 256, 4, 1024], P('shard', None, 'ctx')
- grad_norm_gain: float32 [2, 1024], replicated
- grad_norm_bias: float32 [2, 1024], replicated
- grad_qkv: float32 [1024, 3, 1024], P(('shard', 'ctx'), None, 'tp')
- grad_qv_bias: float32 [2, 1024], P(None, 'tp')
- grad_out: float32 [1024, 1024], P(('shard', 'ctx'), 'tp')
- grad_out_bias: float32 [2, 1024], replicated
- grad_up: float32 [1024, 4096], P(('shard', 'ctx'), 'tp')
- grad_hidden_bias: float32 [4096], P('tp')
- grad_down: float32 [1024, 4096], P(('shard', 'ctx'), 'tp')
The draws below stay inside these ranges and needn't reach their ends.
All inputs are finite; a program needn't handle non-finite values.
Results may differ from the reference program's by a relative error of at most 0.019.
Values may be sent and summed in bfloat16 or wider, within the bound.
A program may use at most 128 MiB of HBM per device.

```python
import math
import jax
import jax.numpy as jnp
from jax import lax

D = 1024
H = 16
HD = 64
FF = 4096
GROUP = 256
LENGTH = 1024
STRIDE = 4
SEQS = 4


def level_of(rng, dims, cuts, low, top_value):
    level = 1.0
    for position, parts in cuts:
        heights = jax.random.uniform(jax.random.fold_in(jax.random.fold_in(rng, 6), position), (parts,), jnp.float32, low / len(cuts), top_value / len(cuts))
        level = level * jnp.repeat(jnp.exp(heights), dims[position] // parts).reshape((-1,) + (1,) * (len(dims) - 1 - position))
    return level


def gaussian(stream_key, extent, scale, limit, cuts=(), kind=jnp.bfloat16):
    drawn = scale * jax.random.normal(stream_key, extent, jnp.float32)
    if cuts:
        drawn = drawn * level_of(stream_key, extent, cuts, -0.22, 0.18)
    return jnp.clip(drawn, -limit, limit).astype(kind)


def setup_inputs(seed: int = 0) -> dict:
    key_list = jax.random.split(jax.random.key(seed), 12)
    tokens = gaussian(key_list[0], (SEQS, GROUP, STRIDE, D), 1.0, 6.0, ((0, 2), (2, 4)))
    cotangent = gaussian(key_list[1], (SEQS, GROUP, STRIDE, D), 1.0, 6.0, ((0, 2), (2, 4)))
    norm_gain = jnp.clip(1.0 + 0.15 * jax.random.normal(key_list[2], (2, D), jnp.float32), 0.25, 1.75).astype(jnp.bfloat16)
    norm_bias = gaussian(key_list[3], (2, D), 0.2, 1.0)
    w_qkv = gaussian(key_list[4], (D, 3, D), D ** -0.5, 0.1875, ((0, 2), (2, 4)))
    qv_bias = gaussian(key_list[5], (2, D), 0.2, 1.0, ((1, 4),))
    w_out = gaussian(key_list[6], (D, D), HD ** -0.5, 0.75, ((0, 2), (1, 4)))
    out_bias = gaussian(key_list[7], (2, D), 0.5, 2.5)
    w_up = gaussian(key_list[8], (D, FF), D ** -0.5, 0.1875, ((0, 2), (1, 4)))
    hidden_bias = gaussian(key_list[9], (FF,), 0.2, 1.0, ((0, 4),))
    w_down = gaussian(key_list[10], (D, FF), FF ** -0.5, 0.09375, ((0, 2), (1, 4)))
    return {"tokens": tokens, "cotangent": cotangent, "norm_gain": norm_gain, "norm_bias": norm_bias, "w_qkv": w_qkv, "qv_bias": qv_bias, "w_out": w_out, "out_bias": out_bias, "w_up": w_up, "hidden_bias": hidden_bias, "w_down": w_down}


EPSILON = 1e-05
HIGHEST = lax.Precision.HIGHEST

@jax.custom_vjp
def low(v):
    return lax.optimization_barrier(v.astype(jnp.bfloat16)).astype(jnp.float32)

@jax.custom_vjp
def low_back(v):
    return v

def low_keep(v):
    return (low(v), None)

def low_pass(kept, grad):
    return (grad,)

def back_keep(v):
    return (v, None)

def back_low(kept, grad):
    return (low(grad),)
low.defvjp(low_keep, low_pass)
low_back.defvjp(back_keep, back_low)

def normalize(values, scale_by, offset):
    average = lax.optimization_barrier(jnp.mean(values, axis=-1, keepdims=True))
    centred = values - average
    spread = lax.optimization_barrier(jnp.mean(centred * centred, axis=-1, keepdims=True))
    return centred * lax.rsqrt(spread + EPSILON) * scale_by + offset

def gelu_tanh(values):
    return jax.nn.gelu(values, approximate=True)

def head_attend(operands):
    query_h, key_h, value_h, slope = operands
    places = jnp.arange(query_h.shape[0], dtype=jnp.int32)
    logits = jnp.dot(query_h, key_h.T, precision=HIGHEST) * (1.0 / math.sqrt(HD))
    distance = (places[:, None] - places[None, :]).astype(jnp.float32)
    logits = low_back(logits - slope * distance)
    allowed = places[None, :] <= places[:, None]
    probs = jax.nn.softmax(jnp.where(allowed, logits, -1e+30), axis=-1)
    return jnp.dot(low(probs), value_h, precision=HIGHEST)

def block_forward(inputs, norm_gain, norm_bias, w_qkv, qv_bias, w_out, out_bias, w_up, hidden_bias, w_down):
    row_count = inputs.shape[0]
    normed_one = low(normalize(inputs, norm_gain[0], norm_bias[0]))
    projected = jnp.einsum('td,dcf->tcf', normed_one, w_qkv, precision=HIGHEST)
    queries = low(low_back(projected[:, 0] + qv_bias[0]))
    key_rows = low(low_back(projected[:, 1]))
    value_rows = low(low_back(projected[:, 2] + qv_bias[1]))

    def to_heads(matrix):
        return matrix.reshape(row_count, H, HD).transpose(1, 0, 2)
    slopes = jnp.exp2(-8.0 * jnp.arange(1, H + 1).astype(jnp.float32) / H)
    heads = lax.map(jax.checkpoint(head_attend), (to_heads(queries), to_heads(key_rows), to_heads(value_rows), slopes))
    attended = low(low_back(heads.transpose(1, 0, 2).reshape(row_count, D)))
    branch = low_back(jnp.dot(attended, w_out.T, precision=HIGHEST))
    resid = inputs + branch + out_bias[0]
    normed_two = low(normalize(resid, norm_gain[1], norm_bias[1]))
    pre_act = low_back(jnp.dot(normed_two, w_up, precision=HIGHEST) + hidden_bias)
    active = low(gelu_tanh(pre_act))
    feed = low_back(jnp.dot(active, w_down.T, precision=HIGHEST))
    return resid + feed + out_bias[1]

def reference(tokens, cotangent, norm_gain, norm_bias, w_qkv, qv_bias, w_out, out_bias, w_up, hidden_bias, w_down):
    params = tuple((weight.astype(jnp.float32) for weight in (norm_gain, norm_bias, w_qkv, qv_bias, w_out, out_bias, w_up, hidden_bias, w_down)))
    inputs = tokens.reshape(SEQS, LENGTH, D).astype(jnp.float32)
    out_grads = cotangent.reshape(SEQS, LENGTH, D).astype(jnp.float32)

    def per_sequence(totals, paired):
        sequence, gradient = paired
        result, pullback = jax.vjp(block_forward, sequence, *params)
        returned = pullback(gradient)
        totals = tuple((former + latter for former, latter in zip(totals, returned[1:])))
        return (totals, (result, returned[0]))
    initial = tuple((jnp.zeros_like(weight) for weight in params))
    totals, (results, input_grads) = lax.scan(per_sequence, initial, (inputs, out_grads))
    layout = (SEQS, GROUP, STRIDE, D)
    return (results.reshape(layout).astype(jnp.bfloat16), input_grads.reshape(layout), totals[0], totals[1], totals[2], totals[3], totals[4], totals[5], totals[6], totals[7], totals[8])
```

```python
import functools
import math

import jax
import jax.numpy as jnp
from jax import lax
from jax.experimental import pallas as pl
from jax.experimental.pallas import tpu as pltpu
from jax.sharding import PartitionSpec as P

H = 16
HD = 64


EPSILON = 1e-05
FLOOR_SCORE = -1e30


def shifted(value, axis, steps):
    count = lax.axis_size(axis)
    pairs = [(source, (source + steps) % count) for source in range(count)]
    return lax.ppermute(value, axis, pairs)


def normalize(values, scale_by, offset):
    average = jnp.mean(values, axis=-1, keepdims=True)
    centred = values - average
    spread = jnp.mean(centred * centred, axis=-1, keepdims=True)
    return centred * lax.rsqrt(spread + EPSILON) * scale_by + offset


def gelu_tanh(values):
    return jax.nn.gelu(values, approximate=True)


def score_block(query_h, key_h, query_pos, key_pos, slopes):
    logits = jnp.einsum("sqhd,skhd->shqk", query_h, key_h, preferred_element_type=jnp.float32) * (
        1.0 / math.sqrt(query_h.shape[-1])
    )
    distance = (query_pos[:, None] - key_pos[None, :]).astype(jnp.float32)
    logits = logits - slopes[None, :, None, None] * distance[None, None]
    allowed = (key_pos[None, :] <= query_pos[:, None])[None, None]
    return (logits, allowed)


def grad_block(query_h, grad_h, log_total, delta_row, query_pos, key_h, value_h, key_pos, slopes):
    scale_by = 1.0 / math.sqrt(query_h.shape[-1])
    logits, allowed = score_block(query_h, key_h, query_pos, key_pos, slopes)
    probs = jnp.where(allowed, jnp.exp(logits - log_total[..., None]), 0.0)
    prob_grad = jnp.einsum("sqhd,skhd->shqk", grad_h, value_h, preferred_element_type=jnp.float32)
    score_grad = (probs * (prob_grad - delta_row[..., None])).astype(jnp.bfloat16)
    query_term = (
        jnp.einsum("shqk,skhd->sqhd", score_grad, key_h, preferred_element_type=jnp.float32)
        * scale_by
    )
    key_term = (
        jnp.einsum("shqk,sqhd->skhd", score_grad, query_h, preferred_element_type=jnp.float32)
        * scale_by
    )
    value_term = jnp.einsum(
        "shqk,sqhd->skhd", probs.astype(jnp.bfloat16), grad_h, preferred_element_type=jnp.float32
    )
    return (query_term, key_term, value_term)


def exchanged(value, axis, mask):
    count = lax.axis_size(axis)
    return lax.ppermute(value, axis, [(source, source ^ mask) for source in range(count)])


def power_of_two(count):
    return count > 1 and count & (count - 1) == 0


def add_bf(left, right):
    return (left.astype(jnp.float32) + right.astype(jnp.float32)).astype(jnp.bfloat16)


def sum_over_tp(partial):
    count = lax.axis_size("tp")
    partial = partial.astype(jnp.bfloat16)
    if not power_of_two(count):
        return lax.psum(partial, "tp").astype(jnp.float32)
    rows = partial.shape[0] // 2
    even = lax.axis_index("tp") % 2 == 0
    low, high = partial[:rows], partial[rows:]
    total = add_bf(
        jnp.where(even, low, high), exchanged(jnp.where(even, high, low), "tp", 1)
    )
    mask = 2
    while mask < count:
        total = add_bf(total, exchanged(total, "tp", mask))
        mask *= 2
    other = exchanged(total, "tp", 1)
    return jnp.concatenate(
        [jnp.where(even, total, other), jnp.where(even, other, total)], 0
    ).astype(jnp.float32)


def sum_small(values, axes):
    flat = jnp.concatenate([value.reshape(-1) for value in values]).reshape(-1, 128)
    for axis in axes:
        count = lax.axis_size(axis)
        if not power_of_two(count):
            flat = lax.psum(flat, axis)
            continue
        mask = 1
        while mask < count:
            flat = flat + exchanged(flat, axis, mask)
            mask *= 2
    flat = flat.reshape(-1)
    results, start = [], 0
    for value in values:
        results.append(flat[start : start + value.size].reshape(value.shape))
        start += value.size
    return results


def whole_rows(block):
    if lax.axis_size("shard") != 2:
        return lax.all_gather(block, "shard", axis=0, tiled=True)
    other = exchanged(block, "shard", 1)
    first = lax.axis_index("shard") == 0
    return jnp.concatenate([jnp.where(first, block, other), jnp.where(first, other, block)], 0)


def outer(left, right):
    return jnp.einsum("td,tf->df", left, right, preferred_element_type=jnp.float32)


def owned_grad(left, right):
    count = lax.axis_size("ctx")
    if lax.axis_size("shard") != 2:
        return lax.psum_scatter(
            outer(left, right), ("shard", "ctx"), scatter_dimension=0, tiled=True
        )
    half_width = left.shape[1] // 2
    shard = lax.axis_index("shard")
    theirs = lax.dynamic_slice_in_dim(left, (1 - shard) * half_width, half_width, 1)
    mine = lax.dynamic_slice_in_dim(left, shard * half_width, half_width, 1)
    half = outer(mine, right) + exchanged(
        outer(theirs, right).astype(jnp.bfloat16), "shard", 1
    ).astype(jnp.float32)
    if count > 8:
        return lax.psum_scatter(half, "ctx", scatter_dimension=0, tiled=True)
    chunks = half.reshape(count, half_width // count, half.shape[1])
    me = lax.axis_index("ctx")

    def chunk(back):
        return lax.dynamic_index_in_dim(
            chunks, lax.rem(me + 2 * count - back, count), 0, keepdims=False
        )

    moving = chunk(1)
    for step in range(count - 1):
        arrived = shifted(moving.astype(jnp.bfloat16), "ctx", 1)
        moving = arrived.astype(jnp.float32) + chunk(step + 2)
    return moving


def spread_heads(groups):
    count = lax.axis_size("ctx")
    me = lax.axis_index("ctx")
    slots = []
    for step in range(count):
        group = lax.dynamic_index_in_dim(groups, lax.rem(me + step, count), 0, keepdims=False)
        slots.append(shifted(group, "ctx", step) if step else group)
    return jnp.stack(slots)


def return_heads(slots):
    count = lax.axis_size("ctx")
    me = lax.axis_index("ctx")
    groups = [shifted(slots[step], "ctx", -step) if step else slots[0] for step in range(count)]
    return lax.dynamic_slice_in_dim(jnp.stack(groups + groups), count - me, count, 0)


def head_parts(ref, column, blocks):
    slots, rows = ref.shape[0], ref.shape[2] // blocks
    return [
        jnp.concatenate(
            [
                ref[slot, 0, block * rows : (block + 1) * rows, column : column + HD]
                for slot in range(slots)
            ],
            0,
        )
        for block in range(blocks)
    ]


def dot_rows(left, right):
    return lax.dot_general(
        left, right, (((1,), (1,)), ((), ())), preferred_element_type=jnp.float32
    )


def dot_plain(left, right):
    return lax.dot_general(
        left, right, (((1,), (0,)), ((), ())), preferred_element_type=jnp.float32
    )


def dot_columns(left, right):
    return lax.dot_general(
        left, right, (((0,), (0,)), ((), ())), preferred_element_type=jnp.float32
    )


def block_weights(query, keys, bias_row, place_row, place_column, scale_by):
    logits = dot_rows(query, keys) * scale_by + bias_row
    logits = jnp.where(place_row <= place_column, logits, FLOOR_SCORE)
    weights = jnp.exp(logits - jnp.max(logits, axis=1, keepdims=True))
    return weights, 1.0 / jnp.sum(weights, axis=1, keepdims=True)


def attend_kernel(blocks, heads, scale_by, bias_ref, row_ref, column_ref, in_ref, out_ref):
    slots, rows = in_ref.shape[0], in_ref.shape[2] // blocks
    size = slots * rows
    for head in range(heads):
        queries, keys, values = (
            head_parts(in_ref, (kind * heads + head) * HD, blocks) for kind in range(3)
        )
        for block in range(blocks):
            reach = (block + 1) * size
            weights, inverse = block_weights(
                queries[block],
                jnp.concatenate(keys[: block + 1], 0),
                bias_ref[head, :, :reach],
                row_ref[:, :reach],
                column_ref[block * size : reach, :],
                scale_by,
            )
            result = (
                dot_plain(
                    weights.astype(jnp.bfloat16), jnp.concatenate(values[: block + 1], 0)
                )
                * inverse
            ).astype(out_ref.dtype)
            for slot in range(slots):
                out_ref[
                    slot, 0, block * rows : (block + 1) * rows, head * HD : (head + 1) * HD
                ] = result[slot * rows : (slot + 1) * rows]


def attend_back_kernel(
    blocks, heads, scale_by, bias_ref, row_ref, column_ref, in_ref, grad_ref, out_ref
):
    slots, rows = in_ref.shape[0], in_ref.shape[2] // blocks
    size = slots * rows

    def store(block, column, value):
        value = value.astype(out_ref.dtype)
        for slot in range(slots):
            out_ref[slot, 0, block * rows : (block + 1) * rows, column : column + HD] = value[
                slot * rows : (slot + 1) * rows
            ]

    for head in range(heads):
        columns = [(kind * heads + head) * HD for kind in range(3)]
        queries, keys, values = (head_parts(in_ref, column, blocks) for column in columns)
        grads = head_parts(grad_ref, head * HD, blocks)
        key_grads, value_grads = [None] * blocks, [None] * blocks
        for block in range(blocks - 1, -1, -1):
            reach = (block + 1) * size
            near_keys = jnp.concatenate(keys[: block + 1], 0)
            weights, inverse = block_weights(
                queries[block],
                near_keys,
                bias_ref[head, :, :reach],
                row_ref[:, :reach],
                column_ref[block * size : reach, :],
                scale_by,
            )
            probs = weights * inverse
            prob_grad = dot_rows(grads[block], jnp.concatenate(values[: block + 1], 0))
            delta = jnp.sum(probs * prob_grad, axis=1, keepdims=True)
            score_grad = (probs * (prob_grad - delta)).astype(jnp.bfloat16)
            store(block, columns[0], dot_plain(score_grad, near_keys) * scale_by)
            key_term = dot_columns(score_grad, queries[block])
            value_term = dot_columns(probs.astype(jnp.bfloat16), grads[block])
            for near in range(block + 1):
                span = slice(near * size, (near + 1) * size)
                if key_grads[near] is None:
                    key_grads[near], value_grads[near] = key_term[span], value_term[span]
                else:
                    key_grads[near] = key_grads[near] + key_term[span]
                    value_grads[near] = value_grads[near] + value_term[span]
        for block in range(blocks):
            store(block, columns[1], key_grads[block] * scale_by)
            store(block, columns[2], value_grads[block])


def head_call(kernel, blocks, heads, tables, arrays, width, flops):
    slots, seqs, rows = arrays[0].shape[:3]

    def table_spec(table):
        return pl.BlockSpec(table.shape, lambda seq: (0,) * table.ndim)

    def slot_spec(columns):
        return pl.BlockSpec((slots, 1, rows, columns), lambda seq: (0, seq, 0, 0))

    return pl.pallas_call(
        functools.partial(kernel, blocks, heads, 1.0 / math.sqrt(HD)),
        grid=(seqs,),
        out_shape=jax.ShapeDtypeStruct((slots, seqs, rows, width), jnp.bfloat16),
        in_specs=[table_spec(table) for table in tables]
        + [slot_spec(array.shape[3]) for array in arrays],
        out_specs=slot_spec(width),
        compiler_params=pltpu.CompilerParams(vmem_limit_bytes=40 * 2**20),
        cost_estimate=pl.CostEstimate(
            flops=flops, bytes_accessed=2 * slots * seqs * rows * 512, transcendentals=0
        ),
    )(*tables, *arrays)


def attend_spread(queries, keys, values, slopes, seqs, rows):
    count = lax.axis_size("ctx")
    me = lax.axis_index("ctx")
    heads = slopes.shape[0] // count
    tokens = seqs * rows
    blocks = 4 if rows % 64 == 0 else 1
    width = heads * HD
    grouped = jnp.stack([queries, keys, values], 1).reshape(tokens, 3, count, width)
    grouped = grouped.transpose(2, 0, 1, 3).reshape(count, tokens, 3 * width)
    spread = spread_heads(grouped).reshape(count, seqs, rows, 3 * width)
    own_slopes = lax.dynamic_slice_in_dim(slopes, me * heads, heads, 0)
    owner = lax.rem(me + count - jnp.arange(count, dtype=jnp.int32), count)
    places = (
        jnp.arange(rows, dtype=jnp.int32).reshape(blocks, 1, rows // blocks) * count
        + owner[None, :, None]
    )
    places = places.reshape(-1).astype(jnp.float32)
    tables = (
        (own_slopes[:, None] * places[None, :])[:, None, :],
        places[None, :],
        places[:, None],
    )
    pairs = heads * seqs * (rows * count) ** 2 * HD
    attended = head_call(
        attend_kernel, blocks, heads, tables, (spread,), width, 3 * pairs
    )

    def homeward(slots, kinds):
        groups = return_heads(slots.reshape(count, tokens, kinds * width))
        groups = groups.reshape(count, tokens, kinds, width).transpose(1, 2, 0, 3)
        return groups.reshape(tokens, kinds, count * width)

    def back(grads):
        grouped_grads = grads.reshape(tokens, count, width).transpose(1, 0, 2)
        spread_grads = spread_heads(grouped_grads).reshape(count, seqs, rows, width)
        slots = head_call(
            attend_back_kernel, blocks, heads, tables, (spread, spread_grads), 3 * width, 8 * pairs
        )
        return homeward(slots, 3)

    return homeward(attended, 1)[:, 0], back


def attend_ring(query_bf, key_bf, value_bf, slopes, seq_dev, group_len):
    tok_rows = seq_dev * group_len
    heads_loc = slopes.shape[0]
    local_width = query_bf.shape[1]
    cycle_size = lax.axis_size("ctx")
    cycle_index = lax.axis_index("ctx")
    positions = jnp.arange(group_len, dtype=jnp.int32)
    own_pos = positions * cycle_size + cycle_index

    def split_heads(matrix):
        return matrix.reshape(seq_dev, group_len, heads_loc, HD)

    query_heads = split_heads(query_bf)
    kv_pair = jnp.stack([key_bf, value_bf], 1).reshape(seq_dev, group_len, 2, local_width)
    kv_single = kv_pair.reshape(seq_dev, group_len, 1, 2, local_width)
    stat_zeros = jnp.zeros((seq_dev, heads_loc, group_len), jnp.float32)
    initial = (
        jnp.full((seq_dev, heads_loc, group_len), FLOOR_SCORE, jnp.float32),
        stat_zeros,
        jnp.zeros((seq_dev, heads_loc, group_len, HD), jnp.float32),
    )
    running = initial
    arrived = lax.all_gather(kv_single, "ctx", axis=2, tiled=True)

    def per_source(running_in, source_step):
        source_block = lax.dynamic_index_in_dim(arrived, source_step, 2, keepdims=False)
        src_keys = split_heads(source_block[:, :, 0])
        src_values = split_heads(source_block[:, :, 1])
        key_pos = positions * cycle_size + source_step
        logits, allowed = score_block(query_heads, src_keys, own_pos, key_pos, slopes)
        run_top, run_total, run_sum = running_in
        row_top = jnp.max(jnp.where(allowed, logits, FLOOR_SCORE), axis=-1)
        fresh_top = jnp.maximum(run_top, row_top)
        weights = jnp.where(allowed, jnp.exp(logits - fresh_top[..., None]), 0.0)
        fade_by = jnp.exp(run_top - fresh_top)
        run_total = run_total * fade_by + jnp.sum(weights, axis=-1)
        run_sum = run_sum * fade_by[..., None] + jnp.einsum(
            "shqk,skhd->shqd",
            weights.astype(jnp.bfloat16),
            src_values,
            preferred_element_type=jnp.float32,
        )
        return ((fresh_top, run_total, run_sum), None)

    running, unused = lax.scan(per_source, running, jnp.arange(arrived.shape[2], dtype=jnp.int32))
    run_top, run_total, run_sum = running
    attended = run_sum / run_total[..., None]
    log_total = run_top + jnp.log(run_total)
    attended_seq = attended.transpose(0, 2, 1, 3)
    attended_bf = attended_seq.reshape(tok_rows, local_width).astype(jnp.bfloat16)

    def back(attend_grad_bf):
        grad_heads = split_heads(attend_grad_bf)
        delta_row = jnp.sum(grad_heads.astype(jnp.float32) * attended_seq, axis=-1).transpose(0, 2, 1)
        head_zeros = jnp.zeros((seq_dev, group_len, heads_loc, HD), jnp.float32)

        def cycle_turn(turn_index, running):
            query_grad, visiting, key_grads = running
            for half_step in range(2):
                source = (cycle_index - 2 * turn_index - half_step) % cycle_size
                key_pos = positions * cycle_size + source
                query_term, key_term, value_term = grad_block(
                    query_heads,
                    grad_heads,
                    log_total,
                    delta_row,
                    own_pos,
                    split_heads(visiting[:, :, 0]),
                    split_heads(visiting[:, :, 1]),
                    key_pos,
                    slopes,
                )
                query_grad = query_grad + query_term
                key_grads = key_grads + jnp.stack(
                    [
                        key_term.reshape(seq_dev, group_len, local_width),
                        value_term.reshape(seq_dev, group_len, local_width),
                    ],
                    2,
                )
                visiting = shifted(visiting, "ctx", 1)
                key_grads = shifted(key_grads.astype(jnp.bfloat16), "ctx", 1).astype(key_grads.dtype)
            return (query_grad, visiting, key_grads)

        pair_zeros = jnp.zeros((seq_dev, group_len, 2, local_width), jnp.float32)
        query_grad, unused, key_grads = lax.fori_loop(
            0, cycle_size // 2, cycle_turn, (head_zeros, kv_pair, pair_zeros)
        )
        return jnp.stack(
            [
                query_grad.reshape(tok_rows, local_width),
                key_grads[:, :, 0].reshape(tok_rows, local_width),
                key_grads[:, :, 1].reshape(tok_rows, local_width),
            ],
            1,
        ).astype(jnp.bfloat16)

    return attended_bf, back


def per_device(
    tokens,
    cotangent,
    norm_gain,
    norm_bias,
    w_qkv,
    qv_bias,
    w_out,
    out_bias,
    w_up,
    hidden_bias,
    w_down,
):
    seq_dev, group_len, model_width = (tokens.shape[0], tokens.shape[1], tokens.shape[3])
    tok_rows = seq_dev * group_len
    local_width = w_qkv.shape[2]
    heads_loc = local_width // HD
    cycle_size = lax.axis_size("ctx")
    slopes = jnp.exp2(
        -8.0
        * (lax.axis_index("tp") * heads_loc + jnp.arange(heads_loc, dtype=jnp.int32) + 1).astype(
            jnp.float32
        )
        / H
    )
    resident = tokens.reshape(tok_rows, model_width).astype(jnp.float32)
    gains = norm_gain.astype(jnp.float32)
    shifts = norm_bias.astype(jnp.float32)
    out_shift = out_bias.astype(jnp.float32)
    qv_shift = qv_bias.astype(jnp.float32)
    hidden_shift = hidden_bias.astype(jnp.float32)
    gathered = (
        whole_rows(w_qkv.reshape(w_qkv.shape[0], 3 * local_width)),
        whole_rows(w_out),
        whole_rows(w_up),
        whole_rows(w_down),
    )
    full_qkv, full_out, full_up, full_down = gathered
    normed_one = normalize(resident, gains[0], shifts[0]).astype(jnp.bfloat16)
    projected = jnp.dot(normed_one, full_qkv, preferred_element_type=jnp.float32)
    projected = projected.reshape(tok_rows, 3, local_width)
    query_bf = (projected[:, 0] + qv_shift[0]).astype(jnp.bfloat16)
    key_bf = projected[:, 1].astype(jnp.bfloat16)
    value_bf = (projected[:, 2] + qv_shift[1]).astype(jnp.bfloat16)
    attend = attend_spread if heads_loc % cycle_size == 0 else attend_ring
    attended_bf, attend_back = attend(query_bf, key_bf, value_bf, slopes, seq_dev, group_len)
    branch = sum_over_tp(
        jnp.einsum("tf,df->td", attended_bf, full_out, preferred_element_type=jnp.float32)
    )
    resid = resident + branch + out_shift[0]
    normed_two = normalize(resid, gains[1], shifts[1]).astype(jnp.bfloat16)
    pre_act = jnp.dot(normed_two, full_up, preferred_element_type=jnp.float32) + hidden_shift
    act_bf = gelu_tanh(pre_act).astype(jnp.bfloat16)
    feed = sum_over_tp(
        jnp.einsum("tf,df->td", act_bf, full_down, preferred_element_type=jnp.float32)
    )
    output = (resid + feed + out_shift[1]).astype(jnp.bfloat16).reshape(tokens.shape)
    back_qkv, back_out, back_up, back_down = gathered
    out_grad = cotangent.reshape(tok_rows, model_width).astype(jnp.float32)
    out_grad_bf = out_grad.astype(jnp.bfloat16)
    grad_down = owned_grad(out_grad_bf, act_bf)
    act_grad = jnp.dot(out_grad_bf, back_down, preferred_element_type=jnp.float32)
    pre_grad = jax.vjp(gelu_tanh, pre_act)[1](act_grad)[0]
    pre_grad_bf = pre_grad.astype(jnp.bfloat16)
    grad_up = owned_grad(normed_two, pre_grad_bf)
    hidden_grad = jnp.sum(pre_grad_bf.astype(jnp.float32), axis=0)
    norm_two_grad = sum_over_tp(
        jnp.einsum("tf,df->td", pre_grad_bf, back_up, preferred_element_type=jnp.float32)
    )
    resid_part, gain_two, shift_two = jax.vjp(normalize, resid, gains[1], shifts[1])[1](
        norm_two_grad
    )
    resid_grad = out_grad + resid_part
    resid_bf = resid_grad.astype(jnp.bfloat16)
    grad_out = owned_grad(resid_bf, attended_bf)
    attend_grad_bf = jnp.dot(resid_bf, back_out, preferred_element_type=jnp.float32).astype(
        jnp.bfloat16
    )
    qkv_grad_bf = attend_back(attend_grad_bf)
    qkv_grad_flat = qkv_grad_bf.reshape(tok_rows, 3 * local_width)
    grad_qkv = owned_grad(normed_one, qkv_grad_flat)
    grad_qkv = grad_qkv.reshape(grad_qkv.shape[0], 3, local_width)
    qv_grad = jnp.stack(
        [
            jnp.sum(qkv_grad_bf[:, 0].astype(jnp.float32), axis=0),
            jnp.sum(qkv_grad_bf[:, 2].astype(jnp.float32), axis=0),
        ]
    )
    norm_one_grad = sum_over_tp(
        jnp.einsum("tf,df->td", qkv_grad_flat, back_qkv, preferred_element_type=jnp.float32)
    )
    input_part, gain_one, shift_one = jax.vjp(normalize, resident, gains[0], shifts[0])[1](
        norm_one_grad
    )
    input_grad = (resid_grad + input_part).reshape(tokens.shape)
    gain_grads = jnp.stack([gain_one, gain_two])
    shift_grads = jnp.stack([shift_one, shift_two])
    out_bias_grad = jnp.stack([jnp.sum(resid_grad, axis=0), jnp.sum(out_grad, axis=0)])
    gain_grads, shift_grads, qv_grad, out_bias_grad, hidden_grad = sum_small(
        (gain_grads, shift_grads, qv_grad, out_bias_grad, hidden_grad), ("shard", "ctx")
    )
    return (
        output,
        input_grad,
        gain_grads,
        shift_grads,
        grad_qkv,
        qv_grad,
        grad_out,
        out_bias_grad,
        grad_up,
        hidden_grad,
        grad_down,
    )


def solution(mesh):
    in_specs = (
        P("shard", None, "ctx", None),
        P("shard", None, "ctx", None),
        P(),
        P(),
        P("shard", None, "tp"),
        P(None, "tp"),
        P("shard", "tp"),
        P(),
        P("shard", "tp"),
        P("tp"),
        P("shard", "tp"),
    )
    out_specs = (
        P("shard", None, "ctx", None),
        P("shard", None, "ctx", None),
        P(),
        P(),
        P(("shard", "ctx"), None, "tp"),
        P(None, "tp"),
        P(("shard", "ctx"), "tp"),
        P(),
        P(("shard", "ctx"), "tp"),
        P("tp"),
        P(("shard", "ctx"), "tp"),
    )
    return jax.shard_map(
        per_device, mesh=mesh, in_specs=in_specs, out_specs=out_specs, check_vma=False
    )
```

```python
import functools
import math

import jax
import jax.numpy as jnp
from jax import lax
from jax.experimental import pallas as pl
from jax.experimental.pallas import tpu as pltpu
from jax.sharding import PartitionSpec as P

H = 16
HD = 64


EPSILON = 1e-05
FLOOR_SCORE = -1e30


def shifted(value, axis, steps):
    count = lax.axis_size(axis)
    pairs = [(source, (source + steps) % count) for source in range(count)]
    return lax.ppermute(value, axis, pairs)


def gelu_tanh(values):
    return jax.nn.gelu(values, approximate=True)


def score_block(query_h, key_h, query_pos, key_pos, slopes):
    logits = jnp.einsum("sqhd,skhd->shqk", query_h, key_h, preferred_element_type=jnp.float32) * (
        1.0 / math.sqrt(query_h.shape[-1])
    )
    distance = (query_pos[:, None] - key_pos[None, :]).astype(jnp.float32)
    logits = logits - slopes[None, :, None, None] * distance[None, None]
    allowed = (key_pos[None, :] <= query_pos[:, None])[None, None]
    return (logits, allowed)


def grad_block(query_h, grad_h, log_total, delta_row, query_pos, key_h, value_h, key_pos, slopes):
    scale_by = 1.0 / math.sqrt(query_h.shape[-1])
    logits, allowed = score_block(query_h, key_h, query_pos, key_pos, slopes)
    probs = jnp.where(allowed, jnp.exp(logits - log_total[..., None]), 0.0)
    prob_grad = jnp.einsum("sqhd,skhd->shqk", grad_h, value_h, preferred_element_type=jnp.float32)
    score_grad = (probs * (prob_grad - delta_row[..., None])).astype(jnp.bfloat16)
    query_term = (
        jnp.einsum("shqk,skhd->sqhd", score_grad, key_h, preferred_element_type=jnp.float32)
        * scale_by
    )
    key_term = (
        jnp.einsum("shqk,sqhd->skhd", score_grad, query_h, preferred_element_type=jnp.float32)
        * scale_by
    )
    value_term = jnp.einsum(
        "shqk,sqhd->skhd", probs.astype(jnp.bfloat16), grad_h, preferred_element_type=jnp.float32
    )
    return (query_term, key_term, value_term)


def exchanged(value, axis, mask):
    count = lax.axis_size(axis)
    return lax.ppermute(value, axis, [(source, source ^ mask) for source in range(count)])


def power_of_two(count):
    return count > 1 and count & (count - 1) == 0


def add_bf(left, right):
    return (left.astype(jnp.float32) + right.astype(jnp.float32)).astype(jnp.bfloat16)


def sum_over_tp(partial):
    count = lax.axis_size("tp")
    partial = partial.astype(jnp.bfloat16)
    if not power_of_two(count):
        return lax.psum(partial, "tp")
    rows = partial.shape[0] // 2
    even = lax.axis_index("tp") % 2 == 0
    low, high = partial[:rows], partial[rows:]
    total = add_bf(
        jnp.where(even, low, high), exchanged(jnp.where(even, high, low), "tp", 1)
    )
    mask = 2
    while mask < count:
        total = add_bf(total, exchanged(total, "tp", mask))
        mask *= 2
    other = exchanged(total, "tp", 1)
    return jnp.concatenate(
        [jnp.where(even, total, other), jnp.where(even, other, total)], 0
    )


def sum_small(values, axes):
    flat = sum_over(
        jnp.concatenate([value.reshape(-1) for value in values]).reshape(-1, 128), axes
    ).reshape(-1)
    results, start = [], 0
    for value in values:
        results.append(flat[start : start + value.size].reshape(value.shape))
        start += value.size
    return results


def sum_over(flat, axes):
    for axis in axes:
        count = lax.axis_size(axis)
        if not power_of_two(count):
            flat = lax.psum(flat, axis)
            continue
        mask = 1
        while mask < count:
            flat = flat + exchanged(flat, axis, mask)
            mask *= 2
    return flat


def whole_rows(block):
    if lax.axis_size("shard") != 2:
        return lax.all_gather(block, "shard", axis=0, tiled=True)
    other = exchanged(block, "shard", 1)
    first = lax.axis_index("shard") == 0
    return jnp.concatenate([jnp.where(first, block, other), jnp.where(first, other, block)], 0)


def outer(left, right):
    return jnp.einsum("td,tf->df", left, right, preferred_element_type=jnp.float32)


def after(value, gate):
    if gate is None:
        return value
    first = gate[(slice(0, 1),) * gate.ndim].reshape((1,) * value.ndim)
    return value + (0.0 * first.astype(jnp.float32)).astype(value.dtype)


def ring_sum(chunk, gates=()):
    count = lax.axis_size("ctx")
    me = lax.axis_index("ctx")
    moving = chunk(lax.rem(me + count - 1, count))
    for step in range(count - 1):
        arrived = shifted(moving.astype(jnp.bfloat16), "ctx", 1)
        term = chunk(lax.rem(me + 2 * count - 2 - step, count))
        gate = gates[step] if step < len(gates) else None
        moving = after(arrived.astype(jnp.float32) + term, gate)
    return moving


def owned_grad(left, right, gate=None):
    count = lax.axis_size("ctx")
    if lax.axis_size("shard") != 2:
        return lax.psum_scatter(
            outer(left, right), ("shard", "ctx"), scatter_dimension=0, tiled=True
        )
    half_width = left.shape[1] // 2
    shard = lax.axis_index("shard")
    theirs = lax.dynamic_slice_in_dim(left, (1 - shard) * half_width, half_width, 1)
    mine = lax.dynamic_slice_in_dim(left, shard * half_width, half_width, 1)
    arrived = exchanged(outer(theirs, right).astype(jnp.bfloat16), "shard", 1)
    half = after(outer(mine, right) + arrived.astype(jnp.float32), gate)
    if count > 8:
        return lax.psum_scatter(half, "ctx", scatter_dimension=0, tiled=True)
    chunks = half.reshape(count, half_width // count, half.shape[1])

    def chunk(member):
        return lax.dynamic_index_in_dim(chunks, member, 0, keepdims=False)

    return ring_sum(chunk)


def owned_grad_ring_first(left, right, gates):
    count = lax.axis_size("ctx")
    if lax.axis_size("shard") != 2 or count > 8:
        return owned_grad(left, right)
    tokens, width = left.shape
    rows = width // (2 * count)
    pieces = left.reshape(tokens, 2, count, rows).transpose(2, 0, 1, 3)
    pieces = pieces.reshape(count, tokens, 2 * rows)

    def chunk(member):
        return outer(lax.dynamic_index_in_dim(pieces, member, 0, keepdims=False), right)

    both = ring_sum(chunk, gates)
    first = lax.axis_index("shard") == 0
    low, high = both[:rows], both[rows:]
    arrived = exchanged(jnp.where(first, high, low).astype(jnp.bfloat16), "shard", 1)
    return jnp.where(first, low, high) + arrived.astype(jnp.float32)


NORM_ROWS = 128


def unit_rows(values):
    average = jnp.mean(values, axis=1, keepdims=True)
    centred = values - average
    inverse = lax.rsqrt(jnp.mean(centred * centred, axis=1, keepdims=True) + EPSILON)
    return centred * inverse, inverse


def rows_back(unit, inverse, grad, gain):
    scaled = grad * gain
    return inverse * (
        scaled
        - jnp.mean(scaled, axis=1, keepdims=True)
        - unit * jnp.mean(scaled * unit, axis=1, keepdims=True)
    )


def row_sum(values):
    return jnp.sum(values, axis=0, keepdims=True)


def add_rows(total_ref, rows):
    @pl.when(pl.program_id(0) == 0)
    def _():
        total_ref[...] = jnp.zeros_like(total_ref)

    for place, row in enumerate(rows):
        total_ref[place : place + 1, :] += row


def norm_one_kernel(gain_ref, shift_ref, x_ref, out_ref):
    unit, _ = unit_rows(x_ref[...].astype(jnp.float32))
    out_ref[...] = (unit * gain_ref[0:1, :] + shift_ref[0:1, :]).astype(out_ref.dtype)


def norm_two_kernel(gain_ref, shift_ref, bias_ref, x_ref, branch_ref, gate_ref, resid_ref, out_ref):
    del gate_ref
    resid = x_ref[...].astype(jnp.float32) + branch_ref[...].astype(jnp.float32) + bias_ref[0:1, :]
    resid_ref[...] = resid
    unit, _ = unit_rows(resid)
    out_ref[...] = (unit * gain_ref[1:2, :] + shift_ref[1:2, :]).astype(out_ref.dtype)


def norm_two_back_kernel(gain_ref, resid_ref, grad_ref, dy_ref, out_ref, out_bf_ref, total_ref):
    unit, inverse = unit_rows(resid_ref[...])
    grad = grad_ref[...].astype(jnp.float32)
    dy = dy_ref[...].astype(jnp.float32)
    result = dy + rows_back(unit, inverse, grad, gain_ref[1:2, :])
    out_ref[...] = result
    out_bf_ref[...] = result.astype(jnp.bfloat16)
    add_rows(total_ref, (row_sum(grad * unit), row_sum(grad), row_sum(result), row_sum(dy)))


def norm_one_sums_kernel(weight_ref, grad_ref, x_ref, out_ref, total_ref):
    unit, _ = unit_rows(x_ref[...].astype(jnp.float32))
    grad = dot_rows(grad_ref[...], weight_ref[...])
    out_ref[...] = grad.astype(jnp.bfloat16)
    add_rows(total_ref, (row_sum(grad * unit), row_sum(grad)))


def norm_one_back_kernel(gain_ref, x_ref, grad_ref, resid_grad_ref, out_ref):
    unit, inverse = unit_rows(x_ref[...].astype(jnp.float32))
    grad = grad_ref[...].astype(jnp.float32)
    out_ref[...] = resid_grad_ref[...] + rows_back(unit, inverse, grad, gain_ref[0:1, :])


def row_call(kernel, whole, by_rows, gates, outs, sums, flops):
    tokens, width = by_rows[-1].shape
    block = NORM_ROWS if tokens % NORM_ROWS == 0 else tokens

    def rows_spec(columns):
        return pl.BlockSpec((block, columns), lambda step: (step, 0))

    def whole_spec(shape):
        return pl.BlockSpec(shape, lambda step: (0,) * len(shape))

    out_shape = [jax.ShapeDtypeStruct((tokens, width), kind) for kind in outs]
    out_specs = [rows_spec(width) for kind in outs]
    if sums:
        out_shape.append(jax.ShapeDtypeStruct((8, width), jnp.float32))
        out_specs.append(whole_spec((8, width)))
    return pl.pallas_call(
        kernel,
        grid=(tokens // block,),
        out_shape=out_shape,
        in_specs=[whole_spec(array.shape) for array in whole]
        + [rows_spec(array.shape[1]) for array in by_rows]
        + [pl.BlockSpec(memory_space=pl.ANY) for gate in gates],
        out_specs=out_specs,
        compiler_params=pltpu.CompilerParams(vmem_limit_bytes=24 * 2**20),
        cost_estimate=pl.CostEstimate(
            flops=flops, bytes_accessed=8 * tokens * width, transcendentals=0
        ),
    )(*whole, *by_rows, *gates)


def spread_heads(groups):
    count = lax.axis_size("ctx")
    me = lax.axis_index("ctx")
    slots = []
    for step in range(count):
        group = lax.dynamic_index_in_dim(groups, lax.rem(me + step, count), 0, keepdims=False)
        slots.append(shifted(group, "ctx", step) if step else group)
    return jnp.stack(slots)


def return_heads(slots):
    count = lax.axis_size("ctx")
    me = lax.axis_index("ctx")
    groups = [shifted(slots[step], "ctx", -step) if step else slots[0] for step in range(count)]
    return lax.dynamic_slice_in_dim(jnp.stack(groups + groups), count - me, count, 0)


def head_parts(ref, column, blocks):
    slots, rows = ref.shape[0], ref.shape[2] // blocks
    return [
        jnp.concatenate(
            [
                ref[slot, 0, block * rows : (block + 1) * rows, column : column + HD]
                for slot in range(slots)
            ],
            0,
        )
        for block in range(blocks)
    ]


def dot_rows(left, right):
    return lax.dot_general(
        left, right, (((1,), (1,)), ((), ())), preferred_element_type=jnp.float32
    )


def dot_plain(left, right):
    return lax.dot_general(
        left, right, (((1,), (0,)), ((), ())), preferred_element_type=jnp.float32
    )


def dot_columns(left, right):
    return lax.dot_general(
        left, right, (((0,), (0,)), ((), ())), preferred_element_type=jnp.float32
    )


def block_weights(query, keys, bias_row, place_row, place_column, scale_by):
    logits = dot_rows(query, keys) * scale_by + bias_row
    logits = jnp.where(place_row <= place_column, logits, FLOOR_SCORE)
    weights = jnp.exp(logits - jnp.max(logits, axis=1, keepdims=True))
    return weights, 1.0 / jnp.sum(weights, axis=1, keepdims=True)


def attend_kernel(
    blocks, heads, scale_by, bias_ref, row_ref, column_ref, in_ref, gate_ref, out_ref
):
    del gate_ref
    slots, rows = in_ref.shape[0], in_ref.shape[2] // blocks
    size = slots * rows
    for head in range(heads):
        queries, keys, values = (
            head_parts(in_ref, (kind * heads + head) * HD, blocks) for kind in range(3)
        )
        for block in range(blocks):
            reach = (block + 1) * size
            weights, inverse = block_weights(
                queries[block],
                jnp.concatenate(keys[: block + 1], 0),
                bias_ref[head, :, :reach],
                row_ref[:, :reach],
                column_ref[block * size : reach, :],
                scale_by,
            )
            result = (
                dot_plain(
                    weights.astype(jnp.bfloat16), jnp.concatenate(values[: block + 1], 0)
                )
                * inverse
            ).astype(out_ref.dtype)
            for slot in range(slots):
                out_ref[
                    slot, 0, block * rows : (block + 1) * rows, head * HD : (head + 1) * HD
                ] = result[slot * rows : (slot + 1) * rows]


def attend_back_kernel(
    blocks, heads, scale_by, bias_ref, row_ref, column_ref, in_ref, grad_ref, out_ref
):
    slots, rows = in_ref.shape[0], in_ref.shape[2] // blocks
    size = slots * rows

    def store(block, column, value):
        value = value.astype(out_ref.dtype)
        for slot in range(slots):
            out_ref[slot, 0, block * rows : (block + 1) * rows, column : column + HD] = value[
                slot * rows : (slot + 1) * rows
            ]

    for head in range(heads):
        columns = [(kind * heads + head) * HD for kind in range(3)]
        queries, keys, values = (head_parts(in_ref, column, blocks) for column in columns)
        grads = head_parts(grad_ref, head * HD, blocks)
        key_grads, value_grads = [None] * blocks, [None] * blocks
        for block in range(blocks - 1, -1, -1):
            reach = (block + 1) * size
            near_keys = jnp.concatenate(keys[: block + 1], 0)
            weights, inverse = block_weights(
                queries[block],
                near_keys,
                bias_ref[head, :, :reach],
                row_ref[:, :reach],
                column_ref[block * size : reach, :],
                scale_by,
            )
            probs = weights * inverse
            prob_grad = dot_rows(grads[block], jnp.concatenate(values[: block + 1], 0))
            delta = jnp.sum(probs * prob_grad, axis=1, keepdims=True)
            score_grad = (probs * (prob_grad - delta)).astype(jnp.bfloat16)
            store(block, columns[0], dot_plain(score_grad, near_keys) * scale_by)
            key_term = dot_columns(score_grad, queries[block])
            value_term = dot_columns(probs.astype(jnp.bfloat16), grads[block])
            for near in range(block + 1):
                span = slice(near * size, (near + 1) * size)
                if key_grads[near] is None:
                    key_grads[near], value_grads[near] = key_term[span], value_term[span]
                else:
                    key_grads[near] = key_grads[near] + key_term[span]
                    value_grads[near] = value_grads[near] + value_term[span]
        for block in range(blocks):
            store(block, columns[1], key_grads[block] * scale_by)
            store(block, columns[2], value_grads[block])


def head_call(kernel, blocks, heads, tables, arrays, gates, width, flops):
    slots, seqs, rows = arrays[0].shape[:3]

    def table_spec(table):
        return pl.BlockSpec(table.shape, lambda seq: (0,) * table.ndim)

    def slot_spec(columns):
        return pl.BlockSpec((slots, 1, rows, columns), lambda seq: (0, seq, 0, 0))

    return pl.pallas_call(
        functools.partial(kernel, blocks, heads, 1.0 / math.sqrt(HD)),
        grid=(seqs,),
        out_shape=jax.ShapeDtypeStruct((slots, seqs, rows, width), jnp.bfloat16),
        in_specs=[table_spec(table) for table in tables]
        + [slot_spec(array.shape[3]) for array in arrays]
        + [pl.BlockSpec(memory_space=pl.ANY) for gate in gates],
        out_specs=slot_spec(width),
        compiler_params=pltpu.CompilerParams(vmem_limit_bytes=40 * 2**20),
        cost_estimate=pl.CostEstimate(
            flops=flops, bytes_accessed=2 * slots * seqs * rows * 512, transcendentals=0
        ),
    )(*tables, *arrays, *gates)


def attend_spread(queries, keys, values, slopes, seqs, rows, gate):
    count = lax.axis_size("ctx")
    me = lax.axis_index("ctx")
    heads = slopes.shape[0] // count
    tokens = seqs * rows
    blocks = 4 if rows % 64 == 0 else 1
    width = heads * HD
    grouped = jnp.stack([queries, keys, values], 1).reshape(tokens, 3, count, width)
    grouped = grouped.transpose(2, 0, 1, 3).reshape(count, tokens, 3 * width)
    spread = spread_heads(grouped).reshape(count, seqs, rows, 3 * width)
    own_slopes = lax.dynamic_slice_in_dim(slopes, me * heads, heads, 0)
    owner = lax.rem(me + count - jnp.arange(count, dtype=jnp.int32), count)
    places = (
        jnp.arange(rows, dtype=jnp.int32).reshape(blocks, 1, rows // blocks) * count
        + owner[None, :, None]
    )
    places = places.reshape(-1).astype(jnp.float32)
    tables = (
        (own_slopes[:, None] * places[None, :])[:, None, :],
        places[None, :],
        places[:, None],
    )
    pairs = heads * seqs * (rows * count) ** 2 * HD
    attended = head_call(
        attend_kernel, blocks, heads, tables, (spread,), (gate,), width, 3 * pairs
    )

    def homeward(slots, kinds):
        groups = return_heads(slots.reshape(count, tokens, kinds * width))
        groups = groups.reshape(count, tokens, kinds, width).transpose(1, 2, 0, 3)
        return groups.reshape(tokens, kinds, count * width)

    def back(grads):
        grouped_grads = grads.reshape(tokens, count, width).transpose(1, 0, 2)
        spread_grads = spread_heads(grouped_grads).reshape(count, seqs, rows, width)
        slots = head_call(
            attend_back_kernel,
            blocks,
            heads,
            tables,
            (spread, spread_grads),
            (),
            3 * width,
            8 * pairs,
        )
        return homeward(slots, 3), slots

    return homeward(attended, 1)[:, 0], back


def attend_ring(query_bf, key_bf, value_bf, slopes, seq_dev, group_len, gate):
    tok_rows = seq_dev * group_len
    heads_loc = slopes.shape[0]
    local_width = query_bf.shape[1]
    cycle_size = lax.axis_size("ctx")
    cycle_index = lax.axis_index("ctx")
    positions = jnp.arange(group_len, dtype=jnp.int32)
    own_pos = positions * cycle_size + cycle_index

    def split_heads(matrix):
        return matrix.reshape(seq_dev, group_len, heads_loc, HD)

    query_heads = split_heads(query_bf)
    kv_pair = jnp.stack([key_bf, value_bf], 1).reshape(seq_dev, group_len, 2, local_width)
    kv_single = kv_pair.reshape(seq_dev, group_len, 1, 2, local_width)
    stat_zeros = jnp.zeros((seq_dev, heads_loc, group_len), jnp.float32)
    initial = (
        jnp.full((seq_dev, heads_loc, group_len), FLOOR_SCORE, jnp.float32),
        stat_zeros,
        jnp.zeros((seq_dev, heads_loc, group_len, HD), jnp.float32),
    )
    running = initial
    arrived = lax.all_gather(kv_single, "ctx", axis=2, tiled=True)

    def per_source(running_in, source_step):
        source_block = lax.dynamic_index_in_dim(arrived, source_step, 2, keepdims=False)
        src_keys = split_heads(source_block[:, :, 0])
        src_values = split_heads(source_block[:, :, 1])
        key_pos = positions * cycle_size + source_step
        logits, allowed = score_block(query_heads, src_keys, own_pos, key_pos, slopes)
        run_top, run_total, run_sum = running_in
        row_top = jnp.max(jnp.where(allowed, logits, FLOOR_SCORE), axis=-1)
        fresh_top = jnp.maximum(run_top, row_top)
        weights = jnp.where(allowed, jnp.exp(logits - fresh_top[..., None]), 0.0)
        fade_by = jnp.exp(run_top - fresh_top)
        run_total = run_total * fade_by + jnp.sum(weights, axis=-1)
        run_sum = run_sum * fade_by[..., None] + jnp.einsum(
            "shqk,skhd->shqd",
            weights.astype(jnp.bfloat16),
            src_values,
            preferred_element_type=jnp.float32,
        )
        return ((fresh_top, run_total, run_sum), None)

    running, unused = lax.scan(per_source, running, jnp.arange(arrived.shape[2], dtype=jnp.int32))
    run_top, run_total, run_sum = running
    attended = run_sum / run_total[..., None]
    log_total = run_top + jnp.log(run_total)
    attended_seq = attended.transpose(0, 2, 1, 3)
    attended_bf = attended_seq.reshape(tok_rows, local_width).astype(jnp.bfloat16)

    def back(attend_grad_bf):
        grad_heads = split_heads(attend_grad_bf)
        delta_row = jnp.sum(grad_heads.astype(jnp.float32) * attended_seq, axis=-1).transpose(0, 2, 1)
        head_zeros = jnp.zeros((seq_dev, group_len, heads_loc, HD), jnp.float32)

        def cycle_turn(turn_index, running):
            query_grad, visiting, key_grads = running
            for half_step in range(2):
                source = (cycle_index - 2 * turn_index - half_step) % cycle_size
                key_pos = positions * cycle_size + source
                query_term, key_term, value_term = grad_block(
                    query_heads,
                    grad_heads,
                    log_total,
                    delta_row,
                    own_pos,
                    split_heads(visiting[:, :, 0]),
                    split_heads(visiting[:, :, 1]),
                    key_pos,
                    slopes,
                )
                query_grad = query_grad + query_term
                key_grads = key_grads + jnp.stack(
                    [
                        key_term.reshape(seq_dev, group_len, local_width),
                        value_term.reshape(seq_dev, group_len, local_width),
                    ],
                    2,
                )
                visiting = shifted(visiting, "ctx", 1)
                key_grads = shifted(key_grads.astype(jnp.bfloat16), "ctx", 1).astype(key_grads.dtype)
            return (query_grad, visiting, key_grads)

        pair_zeros = jnp.zeros((seq_dev, group_len, 2, local_width), jnp.float32)
        query_grad, unused, key_grads = lax.fori_loop(
            0, cycle_size // 2, cycle_turn, (head_zeros, kv_pair, pair_zeros)
        )
        qkv_grad_bf = jnp.stack(
            [
                query_grad.reshape(tok_rows, local_width),
                key_grads[:, :, 0].reshape(tok_rows, local_width),
                key_grads[:, :, 1].reshape(tok_rows, local_width),
            ],
            1,
        ).astype(jnp.bfloat16)
        return qkv_grad_bf, qkv_grad_bf

    return attended_bf, back


def per_device(
    tokens,
    cotangent,
    norm_gain,
    norm_bias,
    w_qkv,
    qv_bias,
    w_out,
    out_bias,
    w_up,
    hidden_bias,
    w_down,
):
    seq_dev, group_len, model_width = (tokens.shape[0], tokens.shape[1], tokens.shape[3])
    tok_rows = seq_dev * group_len
    local_width = w_qkv.shape[2]
    heads_loc = local_width // HD
    cycle_size = lax.axis_size("ctx")
    slopes = jnp.exp2(
        -8.0
        * (lax.axis_index("tp") * heads_loc + jnp.arange(heads_loc, dtype=jnp.int32) + 1).astype(
            jnp.float32
        )
        / H
    )
    x_rows = tokens.reshape(tok_rows, model_width)
    dy_rows = cotangent.reshape(tok_rows, model_width)
    gains = norm_gain.astype(jnp.float32)
    shifts = norm_bias.astype(jnp.float32)
    out_shift = out_bias.astype(jnp.float32)
    qv_shift = qv_bias.astype(jnp.float32)
    hidden_shift = hidden_bias.astype(jnp.float32)
    full_qkv = whole_rows(w_qkv.reshape(w_qkv.shape[0], 3 * local_width))
    full_out = whole_rows(w_out)
    full_up = whole_rows(w_up)
    full_down = whole_rows(w_down)
    row_flops = 16 * tok_rows * model_width
    (normed_one,) = row_call(
        norm_one_kernel, (gains, shifts), (x_rows,), (), (jnp.bfloat16,), False, row_flops
    )
    projected = jnp.dot(normed_one, full_qkv, preferred_element_type=jnp.float32)
    projected = projected.reshape(tok_rows, 3, local_width)
    query_bf = (projected[:, 0] + qv_shift[0]).astype(jnp.bfloat16)
    key_bf = projected[:, 1].astype(jnp.bfloat16)
    value_bf = (projected[:, 2] + qv_shift[1]).astype(jnp.bfloat16)
    attend = attend_spread if heads_loc % cycle_size == 0 else attend_ring
    attended_bf, attend_back = attend(
        query_bf, key_bf, value_bf, slopes, seq_dev, group_len, full_up
    )
    branch = sum_over_tp(
        jnp.einsum("tf,df->td", attended_bf, full_out, preferred_element_type=jnp.float32)
    )
    resid, normed_two = row_call(
        norm_two_kernel,
        (gains, shifts, out_shift),
        (x_rows, branch),
        (full_down,),
        (jnp.float32, jnp.bfloat16),
        False,
        row_flops,
    )
    pre_act = jnp.dot(normed_two, full_up, preferred_element_type=jnp.float32) + hidden_shift
    act_bf = gelu_tanh(pre_act).astype(jnp.bfloat16)
    act_grad = jnp.dot(dy_rows, full_down, preferred_element_type=jnp.float32)
    pre_grad = jax.vjp(gelu_tanh, pre_act)[1](act_grad)[0]
    pre_grad_bf = pre_grad.astype(jnp.bfloat16)
    hidden_grad = jnp.sum(pre_grad_bf.astype(jnp.float32), axis=0)
    norm_two_grad = sum_over_tp(
        jnp.einsum("tf,df->td", pre_grad_bf, full_up, preferred_element_type=jnp.float32)
    )
    resid_grad, resid_bf, sums_two = row_call(
        norm_two_back_kernel,
        (gains,),
        (resid, norm_two_grad, dy_rows),
        (),
        (jnp.float32, jnp.bfloat16),
        True,
        2 * row_flops,
    )
    feed = sum_over_tp(
        after(
            jnp.einsum("tf,df->td", act_bf, full_down, preferred_element_type=jnp.float32),
            resid_bf,
        )
    )
    output = (resid + feed.astype(jnp.float32) + out_shift[1]).astype(jnp.bfloat16)
    output = output.reshape(tokens.shape)
    attend_grad_bf = jnp.dot(resid_bf, full_out, preferred_element_type=jnp.float32).astype(
        jnp.bfloat16
    )
    qkv_grad_bf, attend_done = attend_back(attend_grad_bf)
    qkv_grad_flat = qkv_grad_bf.reshape(tok_rows, 3 * local_width)
    norm_one_part, sums_one = row_call(
        norm_one_sums_kernel,
        (full_qkv,),
        (qkv_grad_flat, x_rows),
        (),
        (jnp.bfloat16,),
        True,
        row_flops + 6 * tok_rows * model_width * local_width,
    )
    norm_one_grad = sum_over_tp(norm_one_part)
    (input_grad,) = row_call(
        norm_one_back_kernel,
        (gains,),
        (x_rows, norm_one_grad, resid_grad),
        (),
        (jnp.float32,),
        False,
        2 * row_flops,
    )
    input_grad = input_grad.reshape(tokens.shape)
    grad_down = owned_grad_ring_first(dy_rows, act_bf, (norm_two_grad, attend_done))
    grad_up = owned_grad(normed_two, pre_grad_bf, attend_done)
    grad_out = owned_grad(resid_bf, attended_bf, qkv_grad_flat)
    grad_qkv = owned_grad(normed_one, qkv_grad_flat)
    grad_qkv = grad_qkv.reshape(grad_qkv.shape[0], 3, local_width)
    qv_grad = jnp.stack(
        [
            jnp.sum(qkv_grad_bf[:, 0].astype(jnp.float32), axis=0),
            jnp.sum(qkv_grad_bf[:, 2].astype(jnp.float32), axis=0),
        ]
    )
    sums_one, sums_two, qv_grad, hidden_grad = sum_small(
        (sums_one[:2], sums_two[:4], qv_grad, hidden_grad), ("shard", "ctx")
    )
    sums_one = sum_over(sums_one, ("tp",))
    gain_grads = jnp.stack([sums_one[0], sums_two[0]])
    shift_grads = jnp.stack([sums_one[1], sums_two[1]])
    out_bias_grad = sums_two[2:4]
    return (
        output,
        input_grad,
        gain_grads,
        shift_grads,
        grad_qkv,
        qv_grad,
        grad_out,
        out_bias_grad,
        grad_up,
        hidden_grad,
        grad_down,
    )


def solution(mesh):
    in_specs = (
        P("shard", None, "ctx", None),
        P("shard", None, "ctx", None),
        P(),
        P(),
        P("shard", None, "tp"),
        P(None, "tp"),
        P("shard", "tp"),
        P(),
        P("shard", "tp"),
        P("tp"),
        P("shard", "tp"),
    )
    out_specs = (
        P("shard", None, "ctx", None),
        P("shard", None, "ctx", None),
        P(),
        P(),
        P(("shard", "ctx"), None, "tp"),
        P(None, "tp"),
        P(("shard", "ctx"), "tp"),
        P(),
        P(("shard", "ctx"), "tp"),
        P("tp"),
        P(("shard", "ctx"), "tp"),
    )
    return jax.shard_map(
        per_device, mesh=mesh, in_specs=in_specs, out_specs=out_specs, check_vma=False
    )
```

```python
import functools
import math

import jax
import jax.numpy as jnp
from jax import lax
from jax.experimental import pallas as pl
from jax.experimental.pallas import tpu as pltpu
from jax.sharding import PartitionSpec as P

H = 16
HD = 64


EPSILON = 1e-05
FLOOR_SCORE = -1e30


def shifted(value, axis, steps):
    count = lax.axis_size(axis)
    pairs = [(source, (source + steps) % count) for source in range(count)]
    return lax.ppermute(value, axis, pairs)


def gelu_tanh(values):
    return jax.nn.gelu(values, approximate=True)


def score_block(query_h, key_h, query_pos, key_pos, slopes):
    logits = jnp.einsum("sqhd,skhd->shqk", query_h, key_h, preferred_element_type=jnp.float32) * (
        1.0 / math.sqrt(query_h.shape[-1])
    )
    distance = (query_pos[:, None] - key_pos[None, :]).astype(jnp.float32)
    logits = logits - slopes[None, :, None, None] * distance[None, None]
    allowed = (key_pos[None, :] <= query_pos[:, None])[None, None]
    return (logits, allowed)


def grad_block(query_h, grad_h, log_total, delta_row, query_pos, key_h, value_h, key_pos, slopes):
    scale_by = 1.0 / math.sqrt(query_h.shape[-1])
    logits, allowed = score_block(query_h, key_h, query_pos, key_pos, slopes)
    probs = jnp.where(allowed, jnp.exp(logits - log_total[..., None]), 0.0)
    prob_grad = jnp.einsum("sqhd,skhd->shqk", grad_h, value_h, preferred_element_type=jnp.float32)
    score_grad = (probs * (prob_grad - delta_row[..., None])).astype(jnp.bfloat16)
    query_term = (
        jnp.einsum("shqk,skhd->sqhd", score_grad, key_h, preferred_element_type=jnp.float32)
        * scale_by
    )
    key_term = (
        jnp.einsum("shqk,sqhd->skhd", score_grad, query_h, preferred_element_type=jnp.float32)
        * scale_by
    )
    value_term = jnp.einsum(
        "shqk,sqhd->skhd", probs.astype(jnp.bfloat16), grad_h, preferred_element_type=jnp.float32
    )
    return (query_term, key_term, value_term)


def exchanged(value, axis, mask):
    count = lax.axis_size(axis)
    return lax.ppermute(value, axis, [(source, source ^ mask) for source in range(count)])


def power_of_two(count):
    return count > 1 and count & (count - 1) == 0


def add_bf(left, right):
    return (left.astype(jnp.float32) + right.astype(jnp.float32)).astype(jnp.bfloat16)


def sum_over_tp(partial):
    count = lax.axis_size("tp")
    partial = partial.astype(jnp.bfloat16)
    if not power_of_two(count):
        return lax.psum(partial, "tp")
    rows = partial.shape[0] // 2
    even = lax.axis_index("tp") % 2 == 0
    low, high = partial[:rows], partial[rows:]
    total = add_bf(
        jnp.where(even, low, high), exchanged(jnp.where(even, high, low), "tp", 1)
    )
    mask = 2
    while mask < count:
        total = add_bf(total, exchanged(total, "tp", mask))
        mask *= 2
    other = exchanged(total, "tp", 1)
    return jnp.concatenate(
        [jnp.where(even, total, other), jnp.where(even, other, total)], 0
    )


SUM_PIECES = 4


def tp_kernel(x_ref, *refs):
    out_ref, first, near, far, total, back, sems = refs[-7:]
    me = lax.axis_index("tp")
    odd = lax.rem(me, 2)
    mate = me + 1 - 2 * odd
    across = lax.rem(me + 2, 4)
    rows = x_ref.shape[0] // 2
    size = rows // SUM_PIECES
    barrier = pltpu.get_barrier_semaphore()
    for partner in (mate, across):
        pl.semaphore_signal(
            barrier, inc=1, device_id={"tp": partner}, device_id_type=pl.DeviceIdType.MESH
        )
    pl.semaphore_wait(barrier, 2)

    def copy(source, target, stage, piece, partner):
        made = pltpu.make_async_remote_copy(
            src_ref=source,
            dst_ref=target,
            send_sem=sems.at[2 * stage, piece],
            recv_sem=sems.at[2 * stage + 1, piece],
            device_id={"tp": partner},
            device_id_type=pl.DeviceIdType.MESH,
        )
        made.start()
        return made

    def span(half, piece):
        return pl.ds(pl.multiple_of(half * rows + piece * size, size), size)

    stages = [[], [], []]
    for piece in range(SUM_PIECES):
        stages[0].append(
            copy(x_ref.at[span(1 - odd, piece), :], first.at[piece], 0, piece, mate)
        )
    for piece in range(SUM_PIECES):
        stages[0][piece].wait_recv()
        near[piece] = add_bf(x_ref[span(odd, piece), :], first[piece])
        stages[1].append(copy(near.at[piece], far.at[piece], 1, piece, across))
    for piece in range(SUM_PIECES):
        stages[1][piece].wait_recv()
        total[piece] = add_bf(near[piece], far[piece])
        stages[2].append(copy(total.at[piece], back.at[piece], 2, piece, mate))
        out_ref[span(odd, piece), :] = total[piece]
    for piece in range(SUM_PIECES):
        stages[2][piece].wait_recv()
        out_ref[span(1 - odd, piece), :] = back[piece]
    for stage in stages:
        for made in stage:
            made.wait_send()


def sum_over_tp_now(partial, gates=()):
    rows, width = partial.shape
    if lax.axis_size("tp") != 4 or rows % (32 * SUM_PIECES) != 0:
        return sum_over_tp(partial)
    piece = pltpu.VMEM((SUM_PIECES, rows // (2 * SUM_PIECES), width), jnp.bfloat16)
    return pl.pallas_call(
        tp_kernel,
        out_shape=jax.ShapeDtypeStruct((rows, width), jnp.bfloat16),
        in_specs=[pl.BlockSpec(memory_space=pltpu.VMEM)]
        + [pl.BlockSpec(memory_space=pl.ANY) for gate in gates],
        out_specs=pl.BlockSpec(memory_space=pltpu.VMEM),
        scratch_shapes=[piece] * 5 + [pltpu.SemaphoreType.DMA((6, SUM_PIECES))],
        compiler_params=pltpu.CompilerParams(
            collective_id=len(gates), has_side_effects=True, vmem_limit_bytes=24 * 2**20
        ),
        cost_estimate=pl.CostEstimate(
            flops=2 * rows * width, bytes_accessed=30 * rows * width, transcendentals=0
        ),
    )(partial.astype(jnp.bfloat16), *gates)


def sum_small(values, axes):
    flat = sum_over(
        jnp.concatenate([value.reshape(-1) for value in values]).reshape(-1, 128), axes
    ).reshape(-1)
    results, start = [], 0
    for value in values:
        results.append(flat[start : start + value.size].reshape(value.shape))
        start += value.size
    return results


def sum_over(flat, axes):
    for axis in axes:
        count = lax.axis_size(axis)
        if not power_of_two(count):
            flat = lax.psum(flat, axis)
            continue
        mask = 1
        while mask < count:
            flat = flat + exchanged(flat, axis, mask)
            mask *= 2
    return flat


def whole_rows(block):
    if lax.axis_size("shard") != 2:
        return lax.all_gather(block, "shard", axis=0, tiled=True)
    other = exchanged(block, "shard", 1)
    first = lax.axis_index("shard") == 0
    return jnp.concatenate([jnp.where(first, block, other), jnp.where(first, other, block)], 0)


def outer(left, right):
    return jnp.einsum("td,tf->df", left, right, preferred_element_type=jnp.float32)


def after(value, gate):
    if gate is None:
        return value
    first = gate[(slice(0, 1),) * gate.ndim].reshape((1,) * value.ndim)
    return value + (0.0 * first.astype(jnp.float32)).astype(value.dtype)


def ring_sum(chunk, gates=(), seen=None):
    count = lax.axis_size("ctx")
    me = lax.axis_index("ctx")
    moving = chunk(lax.rem(me + count - 1, count))
    for step in range(count - 1):
        arrived = shifted(moving.astype(jnp.bfloat16), "ctx", 1)
        term = chunk(lax.rem(me + 2 * count - 2 - step, count))
        gate = gates[step] if step < len(gates) else None
        moving = after(arrived.astype(jnp.float32) + term, gate)
        if seen is not None:
            seen.append(moving)
    return moving


def shard_half(left, right, gate=None):
    if lax.axis_size("shard") != 2:
        return lax.psum_scatter(outer(left, right), "shard", scatter_dimension=0, tiled=True)
    half_width = left.shape[1] // 2
    shard = lax.axis_index("shard")
    theirs = lax.dynamic_slice_in_dim(left, (1 - shard) * half_width, half_width, 1)
    mine = lax.dynamic_slice_in_dim(left, shard * half_width, half_width, 1)
    arrived = exchanged(outer(theirs, right).astype(jnp.bfloat16), "shard", 1)
    return after(outer(mine, right) + arrived.astype(jnp.float32), gate)


def ctx_share(halves, seen=None):
    count = lax.axis_size("ctx")
    if count > 8:
        return [lax.psum_scatter(half, "ctx", scatter_dimension=0, tiled=True) for half in halves]
    rows = halves[0].shape[0] // count

    def chunk(member):
        pieces = [lax.dynamic_slice_in_dim(half, member * rows, rows, 0) for half in halves]
        return pieces[0] if len(pieces) == 1 else jnp.concatenate(pieces, 1)

    total = ring_sum(chunk, (), seen)
    shares, start = [], 0
    for half in halves:
        shares.append(total[:, start : start + half.shape[1]])
        start += half.shape[1]
    return shares


def owned_grad_ring_first(left, right, gates, seen):
    count = lax.axis_size("ctx")
    if lax.axis_size("shard") != 2 or count > 8:
        return ctx_share([shard_half(left, right)])[0]
    tokens, width = left.shape
    rows = width // (2 * count)
    pieces = left.reshape(tokens, 2, count, rows).transpose(2, 0, 1, 3)
    pieces = pieces.reshape(count, tokens, 2 * rows)

    def chunk(member):
        return outer(lax.dynamic_index_in_dim(pieces, member, 0, keepdims=False), right)

    both = ring_sum(chunk, gates, seen)
    first = lax.axis_index("shard") == 0
    low, high = both[:rows], both[rows:]
    arrived = exchanged(jnp.where(first, high, low).astype(jnp.bfloat16), "shard", 1)
    return jnp.where(first, low, high) + arrived.astype(jnp.float32)


NORM_ROWS = 128


def unit_rows(values):
    average = jnp.mean(values, axis=1, keepdims=True)
    centred = values - average
    inverse = lax.rsqrt(jnp.mean(centred * centred, axis=1, keepdims=True) + EPSILON)
    return centred * inverse, inverse


def rows_back(unit, inverse, grad, gain):
    scaled = grad * gain
    return inverse * (
        scaled
        - jnp.mean(scaled, axis=1, keepdims=True)
        - unit * jnp.mean(scaled * unit, axis=1, keepdims=True)
    )


def row_sum(values):
    return jnp.sum(values, axis=0, keepdims=True)


def add_rows(total_ref, rows):
    @pl.when(pl.program_id(0) == 0)
    def _():
        total_ref[...] = jnp.zeros_like(total_ref)

    for place, row in enumerate(rows):
        total_ref[place : place + 1, :] += row


def norm_one_kernel(gain_ref, shift_ref, x_ref, out_ref):
    unit, _ = unit_rows(x_ref[...].astype(jnp.float32))
    out_ref[...] = (unit * gain_ref[0:1, :] + shift_ref[0:1, :]).astype(out_ref.dtype)


def norm_two_kernel(gain_ref, shift_ref, bias_ref, x_ref, branch_ref, gate_ref, resid_ref, out_ref):
    del gate_ref
    resid = x_ref[...].astype(jnp.float32) + branch_ref[...].astype(jnp.float32) + bias_ref[0:1, :]
    resid_ref[...] = resid
    unit, _ = unit_rows(resid)
    out_ref[...] = (unit * gain_ref[1:2, :] + shift_ref[1:2, :]).astype(out_ref.dtype)


def norm_two_back_kernel(gain_ref, resid_ref, grad_ref, dy_ref, out_ref, out_bf_ref, total_ref):
    unit, inverse = unit_rows(resid_ref[...])
    grad = grad_ref[...].astype(jnp.float32)
    dy = dy_ref[...].astype(jnp.float32)
    result = dy + rows_back(unit, inverse, grad, gain_ref[1:2, :])
    out_ref[...] = result
    out_bf_ref[...] = result.astype(jnp.bfloat16)
    add_rows(total_ref, (row_sum(grad * unit), row_sum(grad), row_sum(result), row_sum(dy)))


def norm_one_sums_kernel(weight_ref, grad_ref, x_ref, out_ref, total_ref):
    unit, _ = unit_rows(x_ref[...].astype(jnp.float32))
    grad = dot_rows(grad_ref[...], weight_ref[...])
    out_ref[...] = grad.astype(jnp.bfloat16)
    add_rows(total_ref, (row_sum(grad * unit), row_sum(grad)))


def norm_one_back_kernel(gain_ref, x_ref, grad_ref, resid_grad_ref, out_ref):
    unit, inverse = unit_rows(x_ref[...].astype(jnp.float32))
    grad = grad_ref[...].astype(jnp.float32)
    out_ref[...] = resid_grad_ref[...] + rows_back(unit, inverse, grad, gain_ref[0:1, :])


def row_call(kernel, whole, by_rows, gates, outs, sums, flops):
    tokens, width = by_rows[-1].shape
    block = NORM_ROWS if tokens % NORM_ROWS == 0 else tokens

    def rows_spec(columns):
        return pl.BlockSpec((block, columns), lambda step: (step, 0))

    def whole_spec(shape):
        return pl.BlockSpec(shape, lambda step: (0,) * len(shape))

    out_shape = [jax.ShapeDtypeStruct((tokens, width), kind) for kind in outs]
    out_specs = [rows_spec(width) for kind in outs]
    if sums:
        out_shape.append(jax.ShapeDtypeStruct((8, width), jnp.float32))
        out_specs.append(whole_spec((8, width)))
    return pl.pallas_call(
        kernel,
        grid=(tokens // block,),
        out_shape=out_shape,
        in_specs=[whole_spec(array.shape) for array in whole]
        + [rows_spec(array.shape[1]) for array in by_rows]
        + [pl.BlockSpec(memory_space=pl.ANY) for gate in gates],
        out_specs=out_specs,
        compiler_params=pltpu.CompilerParams(vmem_limit_bytes=24 * 2**20),
        cost_estimate=pl.CostEstimate(
            flops=flops, bytes_accessed=8 * tokens * width, transcendentals=0
        ),
    )(*whole, *by_rows, *gates)


def spread_heads(groups):
    count = lax.axis_size("ctx")
    me = lax.axis_index("ctx")
    slots = []
    for step in range(count):
        group = lax.dynamic_index_in_dim(groups, lax.rem(me + step, count), 0, keepdims=False)
        slots.append(shifted(group, "ctx", step) if step else group)
    return jnp.stack(slots)


def return_heads(slots):
    count = lax.axis_size("ctx")
    me = lax.axis_index("ctx")
    groups = [shifted(slots[step], "ctx", -step) if step else slots[0] for step in range(count)]
    return lax.dynamic_slice_in_dim(jnp.stack(groups + groups), count - me, count, 0)


def head_parts(ref, column, blocks):
    slots, rows = ref.shape[0], ref.shape[2] // blocks
    return [
        jnp.concatenate(
            [
                ref[slot, 0, block * rows : (block + 1) * rows, column : column + HD]
                for slot in range(slots)
            ],
            0,
        )
        for block in range(blocks)
    ]


def dot_rows(left, right):
    return lax.dot_general(
        left, right, (((1,), (1,)), ((), ())), preferred_element_type=jnp.float32
    )


def dot_plain(left, right):
    return lax.dot_general(
        left, right, (((1,), (0,)), ((), ())), preferred_element_type=jnp.float32
    )


def dot_columns(left, right):
    return lax.dot_general(
        left, right, (((0,), (0,)), ((), ())), preferred_element_type=jnp.float32
    )


def block_weights(query, keys, bias_row, place_row, place_column, scale_by):
    logits = dot_rows(query, keys) * scale_by + bias_row
    logits = jnp.where(place_row <= place_column, logits, FLOOR_SCORE)
    weights = jnp.exp(logits - jnp.max(logits, axis=1, keepdims=True))
    return weights, 1.0 / jnp.sum(weights, axis=1, keepdims=True)


def attend_kernel(
    blocks, heads, scale_by, bias_ref, row_ref, column_ref, in_ref, gate_ref, out_ref
):
    del gate_ref
    slots, rows = in_ref.shape[0], in_ref.shape[2] // blocks
    size = slots * rows
    for head in range(heads):
        queries, keys, values = (
            head_parts(in_ref, (kind * heads + head) * HD, blocks) for kind in range(3)
        )
        for block in range(blocks):
            reach = (block + 1) * size
            weights, inverse = block_weights(
                queries[block],
                jnp.concatenate(keys[: block + 1], 0),
                bias_ref[head, :, :reach],
                row_ref[:, :reach],
                column_ref[block * size : reach, :],
                scale_by,
            )
            result = (
                dot_plain(
                    weights.astype(jnp.bfloat16), jnp.concatenate(values[: block + 1], 0)
                )
                * inverse
            ).astype(out_ref.dtype)
            for slot in range(slots):
                out_ref[
                    slot, 0, block * rows : (block + 1) * rows, head * HD : (head + 1) * HD
                ] = result[slot * rows : (slot + 1) * rows]


def attend_back_kernel(
    blocks, heads, scale_by, bias_ref, row_ref, column_ref, in_ref, grad_ref, out_ref
):
    slots, rows = in_ref.shape[0], in_ref.shape[2] // blocks
    size = slots * rows

    def store(block, column, value):
        value = value.astype(out_ref.dtype)
        for slot in range(slots):
            out_ref[slot, 0, block * rows : (block + 1) * rows, column : column + HD] = value[
                slot * rows : (slot + 1) * rows
            ]

    for head in range(heads):
        columns = [(kind * heads + head) * HD for kind in range(3)]
        queries, keys, values = (head_parts(in_ref, column, blocks) for column in columns)
        grads = head_parts(grad_ref, head * HD, blocks)
        key_grads, value_grads = [None] * blocks, [None] * blocks
        for block in range(blocks - 1, -1, -1):
            reach = (block + 1) * size
            near_keys = jnp.concatenate(keys[: block + 1], 0)
            weights, inverse = block_weights(
                queries[block],
                near_keys,
                bias_ref[head, :, :reach],
                row_ref[:, :reach],
                column_ref[block * size : reach, :],
                scale_by,
            )
            probs = weights * inverse
            prob_grad = dot_rows(grads[block], jnp.concatenate(values[: block + 1], 0))
            delta = jnp.sum(probs * prob_grad, axis=1, keepdims=True)
            score_grad = (probs * (prob_grad - delta)).astype(jnp.bfloat16)
            store(block, columns[0], dot_plain(score_grad, near_keys) * scale_by)
            key_term = dot_columns(score_grad, queries[block])
            value_term = dot_columns(probs.astype(jnp.bfloat16), grads[block])
            for near in range(block + 1):
                span = slice(near * size, (near + 1) * size)
                if key_grads[near] is None:
                    key_grads[near], value_grads[near] = key_term[span], value_term[span]
                else:
                    key_grads[near] = key_grads[near] + key_term[span]
                    value_grads[near] = value_grads[near] + value_term[span]
        for block in range(blocks):
            store(block, columns[1], key_grads[block] * scale_by)
            store(block, columns[2], value_grads[block])


def head_call(kernel, blocks, heads, tables, arrays, gates, width, flops):
    slots, seqs, rows = arrays[0].shape[:3]

    def table_spec(table):
        return pl.BlockSpec(table.shape, lambda seq: (0,) * table.ndim)

    def slot_spec(columns):
        return pl.BlockSpec((slots, 1, rows, columns), lambda seq: (0, seq, 0, 0))

    return pl.pallas_call(
        functools.partial(kernel, blocks, heads, 1.0 / math.sqrt(HD)),
        grid=(seqs,),
        out_shape=jax.ShapeDtypeStruct((slots, seqs, rows, width), jnp.bfloat16),
        in_specs=[table_spec(table) for table in tables]
        + [slot_spec(array.shape[3]) for array in arrays]
        + [pl.BlockSpec(memory_space=pl.ANY) for gate in gates],
        out_specs=slot_spec(width),
        compiler_params=pltpu.CompilerParams(vmem_limit_bytes=40 * 2**20),
        cost_estimate=pl.CostEstimate(
            flops=flops, bytes_accessed=2 * slots * seqs * rows * 512, transcendentals=0
        ),
    )(*tables, *arrays, *gates)


def attend_spread(queries, keys, values, slopes, seqs, rows, gate):
    count = lax.axis_size("ctx")
    me = lax.axis_index("ctx")
    heads = slopes.shape[0] // count
    tokens = seqs * rows
    blocks = 4 if rows % 64 == 0 else 1
    width = heads * HD
    grouped = jnp.stack([queries, keys, values], 1).reshape(tokens, 3, count, width)
    grouped = grouped.transpose(2, 0, 1, 3).reshape(count, tokens, 3 * width)
    spread = spread_heads(grouped).reshape(count, seqs, rows, 3 * width)
    own_slopes = lax.dynamic_slice_in_dim(slopes, me * heads, heads, 0)
    owner = lax.rem(me + count - jnp.arange(count, dtype=jnp.int32), count)
    places = (
        jnp.arange(rows, dtype=jnp.int32).reshape(blocks, 1, rows // blocks) * count
        + owner[None, :, None]
    )
    places = places.reshape(-1).astype(jnp.float32)
    tables = (
        (own_slopes[:, None] * places[None, :])[:, None, :],
        places[None, :],
        places[:, None],
    )
    pairs = heads * seqs * (rows * count) ** 2 * HD
    attended = head_call(
        attend_kernel, blocks, heads, tables, (spread,), (gate,), width, 3 * pairs
    )

    def homeward(slots, kinds):
        groups = return_heads(slots.reshape(count, tokens, kinds * width))
        groups = groups.reshape(count, tokens, kinds, width).transpose(1, 2, 0, 3)
        return groups.reshape(tokens, kinds, count * width)

    def back(grads):
        grouped_grads = grads.reshape(tokens, count, width).transpose(1, 0, 2)
        spread_grads = spread_heads(grouped_grads).reshape(count, seqs, rows, width)
        slots = head_call(
            attend_back_kernel,
            blocks,
            heads,
            tables,
            (spread, spread_grads),
            (),
            3 * width,
            8 * pairs,
        )
        return homeward(slots, 3), slots

    return homeward(attended, 1)[:, 0], back


def attend_ring(query_bf, key_bf, value_bf, slopes, seq_dev, group_len, gate):
    tok_rows = seq_dev * group_len
    heads_loc = slopes.shape[0]
    local_width = query_bf.shape[1]
    cycle_size = lax.axis_size("ctx")
    cycle_index = lax.axis_index("ctx")
    positions = jnp.arange(group_len, dtype=jnp.int32)
    own_pos = positions * cycle_size + cycle_index

    def split_heads(matrix):
        return matrix.reshape(seq_dev, group_len, heads_loc, HD)

    query_heads = split_heads(query_bf)
    kv_pair = jnp.stack([key_bf, value_bf], 1).reshape(seq_dev, group_len, 2, local_width)
    kv_single = kv_pair.reshape(seq_dev, group_len, 1, 2, local_width)
    stat_zeros = jnp.zeros((seq_dev, heads_loc, group_len), jnp.float32)
    initial = (
        jnp.full((seq_dev, heads_loc, group_len), FLOOR_SCORE, jnp.float32),
        stat_zeros,
        jnp.zeros((seq_dev, heads_loc, group_len, HD), jnp.float32),
    )
    running = initial
    arrived = lax.all_gather(kv_single, "ctx", axis=2, tiled=True)

    def per_source(running_in, source_step):
        source_block = lax.dynamic_index_in_dim(arrived, source_step, 2, keepdims=False)
        src_keys = split_heads(source_block[:, :, 0])
        src_values = split_heads(source_block[:, :, 1])
        key_pos = positions * cycle_size + source_step
        logits, allowed = score_block(query_heads, src_keys, own_pos, key_pos, slopes)
        run_top, run_total, run_sum = running_in
        row_top = jnp.max(jnp.where(allowed, logits, FLOOR_SCORE), axis=-1)
        fresh_top = jnp.maximum(run_top, row_top)
        weights = jnp.where(allowed, jnp.exp(logits - fresh_top[..., None]), 0.0)
        fade_by = jnp.exp(run_top - fresh_top)
        run_total = run_total * fade_by + jnp.sum(weights, axis=-1)
        run_sum = run_sum * fade_by[..., None] + jnp.einsum(
            "shqk,skhd->shqd",
            weights.astype(jnp.bfloat16),
            src_values,
            preferred_element_type=jnp.float32,
        )
        return ((fresh_top, run_total, run_sum), None)

    running, unused = lax.scan(per_source, running, jnp.arange(arrived.shape[2], dtype=jnp.int32))
    run_top, run_total, run_sum = running
    attended = run_sum / run_total[..., None]
    log_total = run_top + jnp.log(run_total)
    attended_seq = attended.transpose(0, 2, 1, 3)
    attended_bf = attended_seq.reshape(tok_rows, local_width).astype(jnp.bfloat16)

    def back(attend_grad_bf):
        grad_heads = split_heads(attend_grad_bf)
        delta_row = jnp.sum(grad_heads.astype(jnp.float32) * attended_seq, axis=-1).transpose(0, 2, 1)
        head_zeros = jnp.zeros((seq_dev, group_len, heads_loc, HD), jnp.float32)

        def cycle_turn(turn_index, running):
            query_grad, visiting, key_grads = running
            for half_step in range(2):
                source = (cycle_index - 2 * turn_index - half_step) % cycle_size
                key_pos = positions * cycle_size + source
                query_term, key_term, value_term = grad_block(
                    query_heads,
                    grad_heads,
                    log_total,
                    delta_row,
                    own_pos,
                    split_heads(visiting[:, :, 0]),
                    split_heads(visiting[:, :, 1]),
                    key_pos,
                    slopes,
                )
                query_grad = query_grad + query_term
                key_grads = key_grads + jnp.stack(
                    [
                        key_term.reshape(seq_dev, group_len, local_width),
                        value_term.reshape(seq_dev, group_len, local_width),
                    ],
                    2,
                )
                visiting = shifted(visiting, "ctx", 1)
                key_grads = shifted(key_grads.astype(jnp.bfloat16), "ctx", 1).astype(key_grads.dtype)
            return (query_grad, visiting, key_grads)

        pair_zeros = jnp.zeros((seq_dev, group_len, 2, local_width), jnp.float32)
        query_grad, unused, key_grads = lax.fori_loop(
            0, cycle_size // 2, cycle_turn, (head_zeros, kv_pair, pair_zeros)
        )
        qkv_grad_bf = jnp.stack(
            [
                query_grad.reshape(tok_rows, local_width),
                key_grads[:, :, 0].reshape(tok_rows, local_width),
                key_grads[:, :, 1].reshape(tok_rows, local_width),
            ],
            1,
        ).astype(jnp.bfloat16)
        return qkv_grad_bf, qkv_grad_bf

    return attended_bf, back


def per_device(
    tokens,
    cotangent,
    norm_gain,
    norm_bias,
    w_qkv,
    qv_bias,
    w_out,
    out_bias,
    w_up,
    hidden_bias,
    w_down,
):
    seq_dev, group_len, model_width = (tokens.shape[0], tokens.shape[1], tokens.shape[3])
    tok_rows = seq_dev * group_len
    local_width = w_qkv.shape[2]
    heads_loc = local_width // HD
    cycle_size = lax.axis_size("ctx")
    slopes = jnp.exp2(
        -8.0
        * (lax.axis_index("tp") * heads_loc + jnp.arange(heads_loc, dtype=jnp.int32) + 1).astype(
            jnp.float32
        )
        / H
    )
    x_rows = tokens.reshape(tok_rows, model_width)
    dy_rows = cotangent.reshape(tok_rows, model_width)
    gains = norm_gain.astype(jnp.float32)
    shifts = norm_bias.astype(jnp.float32)
    out_shift = out_bias.astype(jnp.float32)
    qv_shift = qv_bias.astype(jnp.float32)
    hidden_shift = hidden_bias.astype(jnp.float32)
    full_qkv = whole_rows(w_qkv.reshape(w_qkv.shape[0], 3 * local_width))
    full_out = whole_rows(w_out)
    full_up = whole_rows(w_up)
    full_down = whole_rows(w_down)
    row_flops = 16 * tok_rows * model_width
    (normed_one,) = row_call(
        norm_one_kernel, (gains, shifts), (x_rows,), (), (jnp.bfloat16,), False, row_flops
    )
    projected = jnp.dot(normed_one, full_qkv, preferred_element_type=jnp.float32)
    projected = projected.reshape(tok_rows, 3, local_width)
    query_bf = (projected[:, 0] + qv_shift[0]).astype(jnp.bfloat16)
    key_bf = projected[:, 1].astype(jnp.bfloat16)
    value_bf = (projected[:, 2] + qv_shift[1]).astype(jnp.bfloat16)
    attend = attend_spread if heads_loc % cycle_size == 0 else attend_ring
    attended_bf, attend_back = attend(
        query_bf, key_bf, value_bf, slopes, seq_dev, group_len, full_out
    )
    branch = sum_over_tp_now(
        after(
            jnp.einsum("tf,df->td", attended_bf, full_out, preferred_element_type=jnp.float32),
            full_up,
        )
    )
    resid, normed_two = row_call(
        norm_two_kernel,
        (gains, shifts, out_shift),
        (x_rows, branch),
        (full_down,),
        (jnp.float32, jnp.bfloat16),
        False,
        row_flops,
    )
    pre_act = jnp.dot(normed_two, full_up, preferred_element_type=jnp.float32) + hidden_shift
    act_bf = gelu_tanh(pre_act).astype(jnp.bfloat16)
    act_grad = jnp.dot(dy_rows, full_down, preferred_element_type=jnp.float32)
    pre_grad = jax.vjp(gelu_tanh, pre_act)[1](act_grad)[0]
    pre_grad_bf = pre_grad.astype(jnp.bfloat16)
    hidden_grad = jnp.sum(pre_grad_bf.astype(jnp.float32), axis=0)
    norm_two_grad = sum_over_tp_now(
        jnp.einsum("tf,df->td", pre_grad_bf, full_up, preferred_element_type=jnp.float32)
    )
    resid_grad, resid_bf, sums_two = row_call(
        norm_two_back_kernel,
        (gains,),
        (resid, norm_two_grad, dy_rows),
        (),
        (jnp.float32, jnp.bfloat16),
        True,
        2 * row_flops,
    )
    feed = sum_over_tp(
        after(
            jnp.einsum("tf,df->td", act_bf, full_down, preferred_element_type=jnp.float32),
            resid_bf,
        )
    )
    output = (resid + feed.astype(jnp.float32) + out_shift[1]).astype(jnp.bfloat16)
    output = output.reshape(tokens.shape)
    attend_grad_bf = jnp.dot(resid_bf, full_out, preferred_element_type=jnp.float32).astype(
        jnp.bfloat16
    )
    qkv_grad_bf, attend_done = attend_back(attend_grad_bf)
    qkv_grad_flat = qkv_grad_bf.reshape(tok_rows, 3 * local_width)
    norm_one_part, sums_one = row_call(
        norm_one_sums_kernel,
        (full_qkv,),
        (qkv_grad_flat, x_rows),
        (),
        (jnp.bfloat16,),
        True,
        row_flops + 6 * tok_rows * model_width * local_width,
    )
    down_seen, up_seen = [], []
    grad_down = owned_grad_ring_first(dy_rows, act_bf, (norm_two_grad, attend_done), down_seen)
    (grad_up,) = ctx_share([shard_half(normed_two, pre_grad_bf, attend_done)], up_seen)
    norm_one_grad = sum_over_tp_now(norm_one_part, tuple(down_seen[-1:] + up_seen[:1]))
    (input_grad,) = row_call(
        norm_one_back_kernel,
        (gains,),
        (x_rows, norm_one_grad, resid_grad),
        (),
        (jnp.float32,),
        False,
        2 * row_flops,
    )
    input_grad = input_grad.reshape(tokens.shape)
    half_out = shard_half(resid_bf, attended_bf)
    half_qkv = shard_half(normed_one, qkv_grad_flat)
    grad_qkv, grad_out = ctx_share([half_qkv, after(half_out, norm_one_grad)])
    grad_qkv = grad_qkv.reshape(grad_qkv.shape[0], 3, local_width)
    qv_grad = jnp.stack(
        [
            jnp.sum(qkv_grad_bf[:, 0].astype(jnp.float32), axis=0),
            jnp.sum(qkv_grad_bf[:, 2].astype(jnp.float32), axis=0),
        ]
    )
    sums_one, sums_two, qv_grad, hidden_grad = sum_small(
        (after(sums_one[:2], norm_one_grad), sums_two[:4], qv_grad, hidden_grad),
        ("shard", "ctx"),
    )
    sums_one = sum_over(sums_one, ("tp",))
    gain_grads = jnp.stack([sums_one[0], sums_two[0]])
    shift_grads = jnp.stack([sums_one[1], sums_two[1]])
    out_bias_grad = sums_two[2:4]
    return (
        output,
        input_grad,
        gain_grads,
        shift_grads,
        grad_qkv,
        qv_grad,
        grad_out,
        out_bias_grad,
        grad_up,
        hidden_grad,
        grad_down,
    )


def solution(mesh):
    in_specs = (
        P("shard", None, "ctx", None),
        P("shard", None, "ctx", None),
        P(),
        P(),
        P("shard", None, "tp"),
        P(None, "tp"),
        P("shard", "tp"),
        P(),
        P("shard", "tp"),
        P("tp"),
        P("shard", "tp"),
    )
    out_specs = (
        P("shard", None, "ctx", None),
        P("shard", None, "ctx", None),
        P(),
        P(),
        P(("shard", "ctx"), None, "tp"),
        P(None, "tp"),
        P(("shard", "ctx"), "tp"),
        P(),
        P(("shard", "ctx"), "tp"),
        P("tp"),
        P(("shard", "ctx"), "tp"),
    )
    return jax.shard_map(
        per_device, mesh=mesh, in_specs=in_specs, out_specs=out_specs, check_vma=False
    )
```

```python
import functools
import math

import jax
import jax.numpy as jnp
from jax import lax
from jax.experimental import pallas as pl
from jax.experimental.pallas import tpu as pltpu
from jax.sharding import PartitionSpec as P

H = 16
HD = 64


EPSILON = 1e-05
FLOOR_SCORE = -1e30


def shifted(value, axis, steps):
    count = lax.axis_size(axis)
    pairs = [(source, (source + steps) % count) for source in range(count)]
    return lax.ppermute(value, axis, pairs)


def gelu_tanh(values):
    return jax.nn.gelu(values, approximate=True)


def score_block(query_h, key_h, query_pos, key_pos, slopes):
    logits = jnp.einsum("sqhd,skhd->shqk", query_h, key_h, preferred_element_type=jnp.float32) * (
        1.0 / math.sqrt(query_h.shape[-1])
    )
    distance = (query_pos[:, None] - key_pos[None, :]).astype(jnp.float32)
    logits = logits - slopes[None, :, None, None] * distance[None, None]
    allowed = (key_pos[None, :] <= query_pos[:, None])[None, None]
    return (logits, allowed)


def grad_block(query_h, grad_h, log_total, delta_row, query_pos, key_h, value_h, key_pos, slopes):
    scale_by = 1.0 / math.sqrt(query_h.shape[-1])
    logits, allowed = score_block(query_h, key_h, query_pos, key_pos, slopes)
    probs = jnp.where(allowed, jnp.exp(logits - log_total[..., None]), 0.0)
    prob_grad = jnp.einsum("sqhd,skhd->shqk", grad_h, value_h, preferred_element_type=jnp.float32)
    score_grad = (probs * (prob_grad - delta_row[..., None])).astype(jnp.bfloat16)
    query_term = (
        jnp.einsum("shqk,skhd->sqhd", score_grad, key_h, preferred_element_type=jnp.float32)
        * scale_by
    )
    key_term = (
        jnp.einsum("shqk,sqhd->skhd", score_grad, query_h, preferred_element_type=jnp.float32)
        * scale_by
    )
    value_term = jnp.einsum(
        "shqk,sqhd->skhd", probs.astype(jnp.bfloat16), grad_h, preferred_element_type=jnp.float32
    )
    return (query_term, key_term, value_term)


def exchanged(value, axis, mask):
    count = lax.axis_size(axis)
    return lax.ppermute(value, axis, [(source, source ^ mask) for source in range(count)])


def power_of_two(count):
    return count > 1 and count & (count - 1) == 0


def add_bf(left, right):
    return (left.astype(jnp.float32) + right.astype(jnp.float32)).astype(jnp.bfloat16)


def sum_over_tp(partial):
    count = lax.axis_size("tp")
    partial = partial.astype(jnp.bfloat16)
    if not power_of_two(count):
        return lax.psum(partial, "tp")
    rows = partial.shape[0] // 2
    even = lax.axis_index("tp") % 2 == 0
    low, high = partial[:rows], partial[rows:]
    total = add_bf(
        jnp.where(even, low, high), exchanged(jnp.where(even, high, low), "tp", 1)
    )
    mask = 2
    while mask < count:
        total = add_bf(total, exchanged(total, "tp", mask))
        mask *= 2
    other = exchanged(total, "tp", 1)
    return jnp.concatenate(
        [jnp.where(even, total, other), jnp.where(even, other, total)], 0
    )


SUM_PIECES = 4


def tp_kernel(x_ref, *refs):
    out_ref, first, near, far, total, back, sems = refs[-7:]
    me = lax.axis_index("tp")
    odd = lax.rem(me, 2)
    mate = me + 1 - 2 * odd
    across = lax.rem(me + 2, 4)
    rows = x_ref.shape[0] // 2
    size = rows // SUM_PIECES
    barrier = pltpu.get_barrier_semaphore()
    for partner in (mate, across):
        pl.semaphore_signal(
            barrier, inc=1, device_id={"tp": partner}, device_id_type=pl.DeviceIdType.MESH
        )
    pl.semaphore_wait(barrier, 2)

    def copy(source, target, stage, piece, partner):
        made = pltpu.make_async_remote_copy(
            src_ref=source,
            dst_ref=target,
            send_sem=sems.at[2 * stage, piece],
            recv_sem=sems.at[2 * stage + 1, piece],
            device_id={"tp": partner},
            device_id_type=pl.DeviceIdType.MESH,
        )
        made.start()
        return made

    def span(half, piece):
        return pl.ds(pl.multiple_of(half * rows + piece * size, size), size)

    stages = [[], [], []]
    for piece in range(SUM_PIECES):
        stages[0].append(
            copy(x_ref.at[span(1 - odd, piece), :], first.at[piece], 0, piece, mate)
        )
    for piece in range(SUM_PIECES):
        stages[0][piece].wait_recv()
        near[piece] = add_bf(x_ref[span(odd, piece), :], first[piece])
        stages[1].append(copy(near.at[piece], far.at[piece], 1, piece, across))
    for piece in range(SUM_PIECES):
        stages[1][piece].wait_recv()
        total[piece] = add_bf(near[piece], far[piece])
        stages[2].append(copy(total.at[piece], back.at[piece], 2, piece, mate))
        out_ref[span(odd, piece), :] = total[piece]
    for piece in range(SUM_PIECES):
        stages[2][piece].wait_recv()
        out_ref[span(1 - odd, piece), :] = back[piece]
    for stage in stages:
        for made in stage:
            made.wait_send()


def sum_over_tp_now(partial, gates=()):
    rows, width = partial.shape
    if lax.axis_size("tp") != 4 or rows % (32 * SUM_PIECES) != 0:
        return sum_over_tp(partial)
    piece = pltpu.VMEM((SUM_PIECES, rows // (2 * SUM_PIECES), width), jnp.bfloat16)
    return pl.pallas_call(
        tp_kernel,
        out_shape=jax.ShapeDtypeStruct((rows, width), jnp.bfloat16),
        in_specs=[pl.BlockSpec(memory_space=pltpu.VMEM)]
        + [pl.BlockSpec(memory_space=pl.ANY) for gate in gates],
        out_specs=pl.BlockSpec(memory_space=pltpu.VMEM),
        scratch_shapes=[piece] * 5 + [pltpu.SemaphoreType.DMA((6, SUM_PIECES))],
        compiler_params=pltpu.CompilerParams(
            collective_id=len(gates), has_side_effects=True, vmem_limit_bytes=24 * 2**20
        ),
        cost_estimate=pl.CostEstimate(
            flops=2 * rows * width, bytes_accessed=30 * rows * width, transcendentals=0
        ),
    )(partial.astype(jnp.bfloat16), *gates)


def sum_small(values, axes):
    flat = sum_over(
        jnp.concatenate([value.reshape(-1) for value in values]).reshape(-1, 128), axes
    ).reshape(-1)
    results, start = [], 0
    for value in values:
        results.append(flat[start : start + value.size].reshape(value.shape))
        start += value.size
    return results


def sum_over(flat, axes):
    for axis in axes:
        count = lax.axis_size(axis)
        if not power_of_two(count):
            flat = lax.psum(flat, axis)
            continue
        mask = 1
        while mask < count:
            flat = flat + exchanged(flat, axis, mask)
            mask *= 2
    return flat


def whole_rows(block):
    if lax.axis_size("shard") != 2:
        return lax.all_gather(block, "shard", axis=0, tiled=True)
    other = exchanged(block, "shard", 1)
    first = lax.axis_index("shard") == 0
    return jnp.concatenate([jnp.where(first, block, other), jnp.where(first, other, block)], 0)


def outer(left, right):
    return jnp.einsum("td,tf->df", left, right, preferred_element_type=jnp.float32)


def after(value, gate):
    if gate is None:
        return value
    first = gate[(slice(0, 1),) * gate.ndim].reshape((1,) * value.ndim)
    return value + (0.0 * first.astype(jnp.float32)).astype(value.dtype)


def ring_sum(chunk, gates=(), seen=None):
    count = lax.axis_size("ctx")
    me = lax.axis_index("ctx")
    moving = chunk(lax.rem(me + count - 1, count))
    for step in range(count - 1):
        arrived = shifted(moving.astype(jnp.bfloat16), "ctx", 1)
        term = chunk(lax.rem(me + 2 * count - 2 - step, count))
        gate = gates[step] if step < len(gates) else None
        moving = after(arrived.astype(jnp.float32) + term, gate)
        if seen is not None:
            seen.append(moving)
    return moving


def shard_half(left, right, gate=None):
    if lax.axis_size("shard") != 2:
        return lax.psum_scatter(outer(left, right), "shard", scatter_dimension=0, tiled=True)
    half_width = left.shape[1] // 2
    shard = lax.axis_index("shard")
    theirs = lax.dynamic_slice_in_dim(left, (1 - shard) * half_width, half_width, 1)
    mine = lax.dynamic_slice_in_dim(left, shard * half_width, half_width, 1)
    arrived = exchanged(outer(theirs, right).astype(jnp.bfloat16), "shard", 1)
    return after(outer(mine, right) + arrived.astype(jnp.float32), gate)


def ctx_share(halves, seen=None):
    count = lax.axis_size("ctx")
    if count > 8:
        return [lax.psum_scatter(half, "ctx", scatter_dimension=0, tiled=True) for half in halves]
    rows = halves[0].shape[0] // count

    def chunk(member):
        pieces = [lax.dynamic_slice_in_dim(half, member * rows, rows, 0) for half in halves]
        return pieces[0] if len(pieces) == 1 else jnp.concatenate(pieces, 1)

    total = ring_sum(chunk, (), seen)
    shares, start = [], 0
    for half in halves:
        shares.append(total[:, start : start + half.shape[1]])
        start += half.shape[1]
    return shares


def owned_grad_ring_first(left, right, gates, seen):
    count = lax.axis_size("ctx")
    if lax.axis_size("shard") != 2 or count > 8:
        return ctx_share([shard_half(left, right)])[0]
    tokens, width = left.shape
    rows = width // (2 * count)
    pieces = left.reshape(tokens, 2, count, rows).transpose(2, 0, 1, 3)
    pieces = pieces.reshape(count, tokens, 2 * rows)

    def chunk(member):
        return outer(lax.dynamic_index_in_dim(pieces, member, 0, keepdims=False), right)

    both = ring_sum(chunk, gates, seen)
    first = lax.axis_index("shard") == 0
    low, high = both[:rows], both[rows:]
    arrived = exchanged(jnp.where(first, high, low).astype(jnp.bfloat16), "shard", 1)
    return jnp.where(first, low, high) + arrived.astype(jnp.float32)


NORM_ROWS = 128


def unit_rows(values):
    average = jnp.mean(values, axis=1, keepdims=True)
    centred = values - average
    inverse = lax.rsqrt(jnp.mean(centred * centred, axis=1, keepdims=True) + EPSILON)
    return centred * inverse, inverse


def rows_back(unit, inverse, grad, gain):
    scaled = grad * gain
    return inverse * (
        scaled
        - jnp.mean(scaled, axis=1, keepdims=True)
        - unit * jnp.mean(scaled * unit, axis=1, keepdims=True)
    )


def row_sum(values):
    return jnp.sum(values, axis=0, keepdims=True)


def add_rows(total_ref, rows):
    @pl.when(pl.program_id(0) == 0)
    def _():
        total_ref[...] = jnp.zeros_like(total_ref)

    for place, row in enumerate(rows):
        total_ref[place : place + 1, :] += row


def norm_one_kernel(gain_ref, shift_ref, x_ref, out_ref):
    unit, _ = unit_rows(x_ref[...].astype(jnp.float32))
    out_ref[...] = (unit * gain_ref[0:1, :] + shift_ref[0:1, :]).astype(out_ref.dtype)


def norm_two_kernel(gain_ref, shift_ref, bias_ref, x_ref, branch_ref, gate_ref, resid_ref, out_ref):
    del gate_ref
    resid = x_ref[...].astype(jnp.float32) + branch_ref[...].astype(jnp.float32) + bias_ref[0:1, :]
    resid_ref[...] = resid
    unit, _ = unit_rows(resid)
    out_ref[...] = (unit * gain_ref[1:2, :] + shift_ref[1:2, :]).astype(out_ref.dtype)


def norm_two_back_kernel(gain_ref, resid_ref, grad_ref, dy_ref, out_ref, out_bf_ref, total_ref):
    unit, inverse = unit_rows(resid_ref[...])
    grad = grad_ref[...].astype(jnp.float32)
    dy = dy_ref[...].astype(jnp.float32)
    result = dy + rows_back(unit, inverse, grad, gain_ref[1:2, :])
    out_ref[...] = result
    out_bf_ref[...] = result.astype(jnp.bfloat16)
    add_rows(total_ref, (row_sum(grad * unit), row_sum(grad), row_sum(result), row_sum(dy)))


def norm_one_sums_kernel(weight_ref, grad_ref, x_ref, *refs):
    out_ref, total_ref = refs[-2:]
    unit, _ = unit_rows(x_ref[...].astype(jnp.float32))
    grad = dot_rows(grad_ref[...], weight_ref[...])
    out_ref[...] = grad.astype(jnp.bfloat16)
    add_rows(total_ref, (row_sum(grad * unit), row_sum(grad)))


def norm_one_back_kernel(gain_ref, x_ref, grad_ref, resid_grad_ref, out_ref):
    unit, inverse = unit_rows(x_ref[...].astype(jnp.float32))
    grad = grad_ref[...].astype(jnp.float32)
    out_ref[...] = resid_grad_ref[...] + rows_back(unit, inverse, grad, gain_ref[0:1, :])


def row_call(kernel, whole, by_rows, gates, outs, sums, flops):
    tokens, width = by_rows[-1].shape
    block = NORM_ROWS if tokens % NORM_ROWS == 0 else tokens

    def rows_spec(columns):
        return pl.BlockSpec((block, columns), lambda step: (step, 0))

    def whole_spec(shape):
        return pl.BlockSpec(shape, lambda step: (0,) * len(shape))

    out_shape = [jax.ShapeDtypeStruct((tokens, width), kind) for kind in outs]
    out_specs = [rows_spec(width) for kind in outs]
    if sums:
        out_shape.append(jax.ShapeDtypeStruct((8, width), jnp.float32))
        out_specs.append(whole_spec((8, width)))
    return pl.pallas_call(
        kernel,
        grid=(tokens // block,),
        out_shape=out_shape,
        in_specs=[whole_spec(array.shape) for array in whole]
        + [rows_spec(array.shape[1]) for array in by_rows]
        + [pl.BlockSpec(memory_space=pl.ANY) for gate in gates],
        out_specs=out_specs,
        compiler_params=pltpu.CompilerParams(vmem_limit_bytes=24 * 2**20),
        cost_estimate=pl.CostEstimate(
            flops=flops, bytes_accessed=8 * tokens * width, transcendentals=0
        ),
    )(*whole, *by_rows, *gates)


def spread_heads(groups):
    count = lax.axis_size("ctx")
    me = lax.axis_index("ctx")
    slots = []
    for step in range(count):
        group = lax.dynamic_index_in_dim(groups, lax.rem(me + step, count), 0, keepdims=False)
        slots.append(shifted(group, "ctx", step) if step else group)
    return jnp.stack(slots)


def return_heads(slots):
    count = lax.axis_size("ctx")
    me = lax.axis_index("ctx")
    groups = [shifted(slots[step], "ctx", -step) if step else slots[0] for step in range(count)]
    return lax.dynamic_slice_in_dim(jnp.stack(groups + groups), count - me, count, 0)


def head_parts(ref, column, blocks):
    slots, rows = ref.shape[0], ref.shape[2] // blocks
    return [
        jnp.concatenate(
            [
                ref[slot, 0, block * rows : (block + 1) * rows, column : column + HD]
                for slot in range(slots)
            ],
            0,
        )
        for block in range(blocks)
    ]


def dot_rows(left, right):
    return lax.dot_general(
        left, right, (((1,), (1,)), ((), ())), preferred_element_type=jnp.float32
    )


def dot_plain(left, right):
    return lax.dot_general(
        left, right, (((1,), (0,)), ((), ())), preferred_element_type=jnp.float32
    )


def dot_columns(left, right):
    return lax.dot_general(
        left, right, (((0,), (0,)), ((), ())), preferred_element_type=jnp.float32
    )


def block_weights(query, keys, bias_row, place_row, place_column, scale_by):
    logits = dot_rows(query, keys) * scale_by + bias_row
    logits = jnp.where(place_row <= place_column, logits, FLOOR_SCORE)
    weights = jnp.exp(logits - jnp.max(logits, axis=1, keepdims=True))
    return weights, 1.0 / jnp.sum(weights, axis=1, keepdims=True)


def attend_kernel(
    blocks, heads, scale_by, bias_ref, row_ref, column_ref, in_ref, gate_ref, out_ref
):
    del gate_ref
    slots, rows = in_ref.shape[0], in_ref.shape[2] // blocks
    size = slots * rows
    for head in range(heads):
        queries, keys, values = (
            head_parts(in_ref, (kind * heads + head) * HD, blocks) for kind in range(3)
        )
        for block in range(blocks):
            reach = (block + 1) * size
            weights, inverse = block_weights(
                queries[block],
                jnp.concatenate(keys[: block + 1], 0),
                bias_ref[head, :, :reach],
                row_ref[:, :reach],
                column_ref[block * size : reach, :],
                scale_by,
            )
            result = (
                dot_plain(
                    weights.astype(jnp.bfloat16), jnp.concatenate(values[: block + 1], 0)
                )
                * inverse
            ).astype(out_ref.dtype)
            for slot in range(slots):
                out_ref[
                    slot, 0, block * rows : (block + 1) * rows, head * HD : (head + 1) * HD
                ] = result[slot * rows : (slot + 1) * rows]


def attend_back_kernel(
    blocks, heads, scale_by, bias_ref, row_ref, column_ref, in_ref, grad_ref, *refs
):
    out_ref = refs[-1]
    slots, rows = in_ref.shape[0], in_ref.shape[2] // blocks
    size = slots * rows

    def store(block, column, value):
        value = value.astype(out_ref.dtype)
        for slot in range(slots):
            out_ref[slot, 0, block * rows : (block + 1) * rows, column : column + HD] = value[
                slot * rows : (slot + 1) * rows
            ]

    for head in range(heads):
        columns = [(kind * heads + head) * HD for kind in range(3)]
        queries, keys, values = (head_parts(in_ref, column, blocks) for column in columns)
        grads = head_parts(grad_ref, head * HD, blocks)
        key_grads, value_grads = [None] * blocks, [None] * blocks
        for block in range(blocks - 1, -1, -1):
            reach = (block + 1) * size
            near_keys = jnp.concatenate(keys[: block + 1], 0)
            weights, inverse = block_weights(
                queries[block],
                near_keys,
                bias_ref[head, :, :reach],
                row_ref[:, :reach],
                column_ref[block * size : reach, :],
                scale_by,
            )
            probs = weights * inverse
            prob_grad = dot_rows(grads[block], jnp.concatenate(values[: block + 1], 0))
            delta = jnp.sum(probs * prob_grad, axis=1, keepdims=True)
            score_grad = (probs * (prob_grad - delta)).astype(jnp.bfloat16)
            store(block, columns[0], dot_plain(score_grad, near_keys) * scale_by)
            key_term = dot_columns(score_grad, queries[block])
            value_term = dot_columns(probs.astype(jnp.bfloat16), grads[block])
            for near in range(block + 1):
                span = slice(near * size, (near + 1) * size)
                if key_grads[near] is None:
                    key_grads[near], value_grads[near] = key_term[span], value_term[span]
                else:
                    key_grads[near] = key_grads[near] + key_term[span]
                    value_grads[near] = value_grads[near] + value_term[span]
        for block in range(blocks):
            store(block, columns[1], key_grads[block] * scale_by)
            store(block, columns[2], value_grads[block])


def head_call(kernel, blocks, heads, tables, arrays, gates, width, flops):
    slots, seqs, rows = arrays[0].shape[:3]

    def table_spec(table):
        return pl.BlockSpec(table.shape, lambda seq: (0,) * table.ndim)

    def slot_spec(columns):
        return pl.BlockSpec((slots, 1, rows, columns), lambda seq: (0, seq, 0, 0))

    return pl.pallas_call(
        functools.partial(kernel, blocks, heads, 1.0 / math.sqrt(HD)),
        grid=(seqs,),
        out_shape=jax.ShapeDtypeStruct((slots, seqs, rows, width), jnp.bfloat16),
        in_specs=[table_spec(table) for table in tables]
        + [slot_spec(array.shape[3]) for array in arrays]
        + [pl.BlockSpec(memory_space=pl.ANY) for gate in gates],
        out_specs=slot_spec(width),
        compiler_params=pltpu.CompilerParams(vmem_limit_bytes=40 * 2**20),
        cost_estimate=pl.CostEstimate(
            flops=flops, bytes_accessed=2 * slots * seqs * rows * 512, transcendentals=0
        ),
    )(*tables, *arrays, *gates)


def attend_spread(queries, keys, values, slopes, seqs, rows, gate):
    count = lax.axis_size("ctx")
    me = lax.axis_index("ctx")
    heads = slopes.shape[0] // count
    tokens = seqs * rows
    blocks = 4 if rows % 64 == 0 else 1
    width = heads * HD
    grouped = jnp.stack([queries, keys, values], 1).reshape(tokens, 3, count, width)
    grouped = grouped.transpose(2, 0, 1, 3).reshape(count, tokens, 3 * width)
    spread = spread_heads(grouped).reshape(count, seqs, rows, 3 * width)
    own_slopes = lax.dynamic_slice_in_dim(slopes, me * heads, heads, 0)
    owner = lax.rem(me + count - jnp.arange(count, dtype=jnp.int32), count)
    places = (
        jnp.arange(rows, dtype=jnp.int32).reshape(blocks, 1, rows // blocks) * count
        + owner[None, :, None]
    )
    places = places.reshape(-1).astype(jnp.float32)
    tables = (
        (own_slopes[:, None] * places[None, :])[:, None, :],
        places[None, :],
        places[:, None],
    )
    pairs = heads * seqs * (rows * count) ** 2 * HD
    attended = head_call(
        attend_kernel, blocks, heads, tables, (spread,), (gate,), width, 3 * pairs
    )

    def homeward(slots, kinds):
        groups = return_heads(slots.reshape(count, tokens, kinds * width))
        groups = groups.reshape(count, tokens, kinds, width).transpose(1, 2, 0, 3)
        return groups.reshape(tokens, kinds, count * width)

    def back(grads, gates):
        grouped_grads = grads.reshape(tokens, count, width).transpose(1, 0, 2)
        spread_grads = spread_heads(grouped_grads).reshape(count, seqs, rows, width)
        slots = head_call(
            attend_back_kernel,
            blocks,
            heads,
            tables,
            (spread, spread_grads),
            gates,
            3 * width,
            8 * pairs,
        )
        return homeward(slots, 3)

    return homeward(attended, 1)[:, 0], back


def attend_ring(query_bf, key_bf, value_bf, slopes, seq_dev, group_len, gate):
    tok_rows = seq_dev * group_len
    heads_loc = slopes.shape[0]
    local_width = query_bf.shape[1]
    cycle_size = lax.axis_size("ctx")
    cycle_index = lax.axis_index("ctx")
    positions = jnp.arange(group_len, dtype=jnp.int32)
    own_pos = positions * cycle_size + cycle_index

    def split_heads(matrix):
        return matrix.reshape(seq_dev, group_len, heads_loc, HD)

    query_heads = split_heads(query_bf)
    kv_pair = jnp.stack([key_bf, value_bf], 1).reshape(seq_dev, group_len, 2, local_width)
    kv_single = kv_pair.reshape(seq_dev, group_len, 1, 2, local_width)
    stat_zeros = jnp.zeros((seq_dev, heads_loc, group_len), jnp.float32)
    initial = (
        jnp.full((seq_dev, heads_loc, group_len), FLOOR_SCORE, jnp.float32),
        stat_zeros,
        jnp.zeros((seq_dev, heads_loc, group_len, HD), jnp.float32),
    )
    running = initial
    arrived = lax.all_gather(kv_single, "ctx", axis=2, tiled=True)

    def per_source(running_in, source_step):
        source_block = lax.dynamic_index_in_dim(arrived, source_step, 2, keepdims=False)
        src_keys = split_heads(source_block[:, :, 0])
        src_values = split_heads(source_block[:, :, 1])
        key_pos = positions * cycle_size + source_step
        logits, allowed = score_block(query_heads, src_keys, own_pos, key_pos, slopes)
        run_top, run_total, run_sum = running_in
        row_top = jnp.max(jnp.where(allowed, logits, FLOOR_SCORE), axis=-1)
        fresh_top = jnp.maximum(run_top, row_top)
        weights = jnp.where(allowed, jnp.exp(logits - fresh_top[..., None]), 0.0)
        fade_by = jnp.exp(run_top - fresh_top)
        run_total = run_total * fade_by + jnp.sum(weights, axis=-1)
        run_sum = run_sum * fade_by[..., None] + jnp.einsum(
            "shqk,skhd->shqd",
            weights.astype(jnp.bfloat16),
            src_values,
            preferred_element_type=jnp.float32,
        )
        return ((fresh_top, run_total, run_sum), None)

    running, unused = lax.scan(per_source, running, jnp.arange(arrived.shape[2], dtype=jnp.int32))
    run_top, run_total, run_sum = running
    attended = run_sum / run_total[..., None]
    log_total = run_top + jnp.log(run_total)
    attended_seq = attended.transpose(0, 2, 1, 3)
    attended_bf = attended_seq.reshape(tok_rows, local_width).astype(jnp.bfloat16)

    def back(attend_grad_bf, gates):
        del gates
        grad_heads = split_heads(attend_grad_bf)
        delta_row = jnp.sum(grad_heads.astype(jnp.float32) * attended_seq, axis=-1).transpose(0, 2, 1)
        head_zeros = jnp.zeros((seq_dev, group_len, heads_loc, HD), jnp.float32)

        def cycle_turn(turn_index, running):
            query_grad, visiting, key_grads = running
            for half_step in range(2):
                source = (cycle_index - 2 * turn_index - half_step) % cycle_size
                key_pos = positions * cycle_size + source
                query_term, key_term, value_term = grad_block(
                    query_heads,
                    grad_heads,
                    log_total,
                    delta_row,
                    own_pos,
                    split_heads(visiting[:, :, 0]),
                    split_heads(visiting[:, :, 1]),
                    key_pos,
                    slopes,
                )
                query_grad = query_grad + query_term
                key_grads = key_grads + jnp.stack(
                    [
                        key_term.reshape(seq_dev, group_len, local_width),
                        value_term.reshape(seq_dev, group_len, local_width),
                    ],
                    2,
                )
                visiting = shifted(visiting, "ctx", 1)
                key_grads = shifted(key_grads.astype(jnp.bfloat16), "ctx", 1).astype(key_grads.dtype)
            return (query_grad, visiting, key_grads)

        pair_zeros = jnp.zeros((seq_dev, group_len, 2, local_width), jnp.float32)
        query_grad, unused, key_grads = lax.fori_loop(
            0, cycle_size // 2, cycle_turn, (head_zeros, kv_pair, pair_zeros)
        )
        qkv_grad_bf = jnp.stack(
            [
                query_grad.reshape(tok_rows, local_width),
                key_grads[:, :, 0].reshape(tok_rows, local_width),
                key_grads[:, :, 1].reshape(tok_rows, local_width),
            ],
            1,
        ).astype(jnp.bfloat16)
        return qkv_grad_bf

    return attended_bf, back


def per_device(
    tokens,
    cotangent,
    norm_gain,
    norm_bias,
    w_qkv,
    qv_bias,
    w_out,
    out_bias,
    w_up,
    hidden_bias,
    w_down,
):
    seq_dev, group_len, model_width = (tokens.shape[0], tokens.shape[1], tokens.shape[3])
    tok_rows = seq_dev * group_len
    local_width = w_qkv.shape[2]
    heads_loc = local_width // HD
    cycle_size = lax.axis_size("ctx")
    slopes = jnp.exp2(
        -8.0
        * (lax.axis_index("tp") * heads_loc + jnp.arange(heads_loc, dtype=jnp.int32) + 1).astype(
            jnp.float32
        )
        / H
    )
    x_rows = tokens.reshape(tok_rows, model_width)
    dy_rows = cotangent.reshape(tok_rows, model_width)
    gains = norm_gain.astype(jnp.float32)
    shifts = norm_bias.astype(jnp.float32)
    out_shift = out_bias.astype(jnp.float32)
    qv_shift = qv_bias.astype(jnp.float32)
    hidden_shift = hidden_bias.astype(jnp.float32)
    full_qkv = whole_rows(w_qkv.reshape(w_qkv.shape[0], 3 * local_width))
    full_out = whole_rows(w_out)
    full_up = whole_rows(w_up)
    full_down = whole_rows(w_down)
    row_flops = 16 * tok_rows * model_width
    (normed_one,) = row_call(
        norm_one_kernel, (gains, shifts), (x_rows,), (), (jnp.bfloat16,), False, row_flops
    )
    projected = jnp.dot(normed_one, full_qkv, preferred_element_type=jnp.float32)
    projected = projected.reshape(tok_rows, 3, local_width)
    query_bf = (projected[:, 0] + qv_shift[0]).astype(jnp.bfloat16)
    key_bf = projected[:, 1].astype(jnp.bfloat16)
    value_bf = (projected[:, 2] + qv_shift[1]).astype(jnp.bfloat16)
    attend = attend_spread if heads_loc % cycle_size == 0 else attend_ring
    attended_bf, attend_back = attend(
        query_bf, key_bf, value_bf, slopes, seq_dev, group_len, full_out
    )
    branch = sum_over_tp_now(
        after(
            jnp.einsum("tf,df->td", attended_bf, full_out, preferred_element_type=jnp.float32),
            full_up,
        )
    )
    resid, normed_two = row_call(
        norm_two_kernel,
        (gains, shifts, out_shift),
        (x_rows, branch),
        (full_down,),
        (jnp.float32, jnp.bfloat16),
        False,
        row_flops,
    )
    pre_act = jnp.dot(normed_two, full_up, preferred_element_type=jnp.float32) + hidden_shift
    act_bf = gelu_tanh(pre_act).astype(jnp.bfloat16)
    act_grad = jnp.dot(dy_rows, full_down, preferred_element_type=jnp.float32)
    pre_grad = jax.vjp(gelu_tanh, pre_act)[1](act_grad)[0]
    pre_grad_bf = pre_grad.astype(jnp.bfloat16)
    hidden_grad = jnp.sum(pre_grad_bf.astype(jnp.float32), axis=0)
    norm_two_grad = sum_over_tp_now(
        jnp.einsum("tf,df->td", pre_grad_bf, full_up, preferred_element_type=jnp.float32)
    )
    resid_grad, resid_bf, sums_two = row_call(
        norm_two_back_kernel,
        (gains,),
        (resid, norm_two_grad, dy_rows),
        (),
        (jnp.float32, jnp.bfloat16),
        True,
        2 * row_flops,
    )
    feed = sum_over_tp(
        after(
            jnp.einsum("tf,df->td", act_bf, full_down, preferred_element_type=jnp.float32),
            resid_bf,
        )
    )
    output = (resid + feed.astype(jnp.float32) + out_shift[1]).astype(jnp.bfloat16)
    output = output.reshape(tokens.shape)
    attend_grad_bf = jnp.dot(resid_bf, full_out, preferred_element_type=jnp.float32).astype(
        jnp.bfloat16
    )
    down_seen, up_seen = [], []
    grad_down = owned_grad_ring_first(dy_rows, act_bf, (norm_two_grad,), down_seen)
    half_up = shard_half(normed_two, pre_grad_bf)
    (grad_up,) = ctx_share([half_up], up_seen)
    qkv_grad_bf = attend_back(attend_grad_bf, tuple(down_seen[:1]) + (half_up,))
    qkv_grad_flat = qkv_grad_bf.reshape(tok_rows, 3 * local_width)
    norm_one_part, sums_one = row_call(
        norm_one_sums_kernel,
        (full_qkv,),
        (qkv_grad_flat, x_rows),
        tuple(down_seen[1:2] + up_seen[:1]),
        (jnp.bfloat16,),
        True,
        row_flops + 6 * tok_rows * model_width * local_width,
    )
    norm_one_grad = sum_over_tp_now(norm_one_part)
    (input_grad,) = row_call(
        norm_one_back_kernel,
        (gains,),
        (x_rows, norm_one_grad, resid_grad),
        (),
        (jnp.float32,),
        False,
        2 * row_flops,
    )
    input_grad = input_grad.reshape(tokens.shape)
    half_out = shard_half(resid_bf, attended_bf)
    half_qkv = shard_half(normed_one, qkv_grad_flat)
    grad_qkv, grad_out = ctx_share([half_qkv, after(half_out, norm_one_grad)])
    grad_qkv = grad_qkv.reshape(grad_qkv.shape[0], 3, local_width)
    qv_grad = jnp.stack(
        [
            jnp.sum(qkv_grad_bf[:, 0].astype(jnp.float32), axis=0),
            jnp.sum(qkv_grad_bf[:, 2].astype(jnp.float32), axis=0),
        ]
    )
    sums_one, sums_two, qv_grad, hidden_grad = sum_small(
        (after(sums_one[:2], norm_one_grad), sums_two[:4], qv_grad, hidden_grad),
        ("shard", "ctx"),
    )
    sums_one = sum_over(sums_one, ("tp",))
    gain_grads = jnp.stack([sums_one[0], sums_two[0]])
    shift_grads = jnp.stack([sums_one[1], sums_two[1]])
    out_bias_grad = sums_two[2:4]
    return (
        output,
        input_grad,
        gain_grads,
        shift_grads,
        grad_qkv,
        qv_grad,
        grad_out,
        out_bias_grad,
        grad_up,
        hidden_grad,
        grad_down,
    )


def solution(mesh):
    in_specs = (
        P("shard", None, "ctx", None),
        P("shard", None, "ctx", None),
        P(),
        P(),
        P("shard", None, "tp"),
        P(None, "tp"),
        P("shard", "tp"),
        P(),
        P("shard", "tp"),
        P("tp"),
        P("shard", "tp"),
    )
    out_specs = (
        P("shard", None, "ctx", None),
        P("shard", None, "ctx", None),
        P(),
        P(),
        P(("shard", "ctx"), None, "tp"),
        P(None, "tp"),
        P(("shard", "ctx"), "tp"),
        P(),
        P(("shard", "ctx"), "tp"),
        P("tp"),
        P(("shard", "ctx"), "tp"),
    )
    return jax.shard_map(
        per_device, mesh=mesh, in_specs=in_specs, out_specs=out_specs, check_vma=False
    )
```
